768 devices in a mesh: dom: 192 (over y, z, core), grp: 4 (over x).
Axes of the slice: x: 4, y: 8, z: 12, core: 2. Of those that a mesh axis runs over, the one named last changes fastest.
Arguments:
- trace: float32 [192, 4, 72, 1280], P('dom', 'grp'), may hold values from -6 to 6
- rhs: float32 [192, 4, 72, 1280], P('dom', 'grp'), may hold values from -6 to 6
- stiffness: float32 [192, 4, 32, 25600], P('dom', 'grp'), may hold values from -0.5 to 0.5
- elem_faces: int32 [192, 4, 32, 4], P('dom', 'grp'), may hold values from 0 to 79, as said below
- orient: int32 [192, 4, 32, 4], P('dom', 'grp'), may hold values from 0 to 5
- counts: int32 [192, 4], P('dom', 'grp'), may hold values from 4 to 8, as said below
Outputs:
- condensed: float32 [192, 4, 80, 1280], P('dom', 'grp')
- coarse: float32 [192, 288, 384], P('dom')
The draws below stay inside these ranges and needn't reach their ends.
Inputs may be any that keep to these rules, and one draw needn't show every extreme that they name: counts[d, g] of the 8 slots shared by partitions (d, g) and (d + 1, g) are used, slots 0 to counts[d, g] - 1; some partition uses all 8. `elem_faces`: each interior slot is named once or twice; owned slot 64 + j is named exactly once when j < counts[d, g] and never otherwise; lower slot 72 + j is named exactly once when j < counts[d - 1, g] and never otherwise (on d = 0, with the counts of the last partition along dom, naming faces on the outer boundary).
All inputs are finite; a program needn't handle non-finite values.
Results may differ from the reference program's by a relative error of at most 0.0003.
Values sent between devices are 32-bit elements; how exact they have to be, the bound alone decides.
A program may use at most 32 MiB of HBM per device.

```python
import jax
import jax.numpy as jnp
import numpy as np
from jax import lax

ELEMS = 32
NODES = 10
FIELDS = 4
RHS = 32
VERTS = 3
INNER = 64
PAIR = 8
F_OWN = 72
ROW = 1280
TRACE = 160
N_DOM = 192
N_GRP = 4


def pair_counts(key):
    key = jax.random.fold_in(key, 17)
    base_key, pick_key = jax.random.split(key)
    partitions = N_DOM * N_GRP
    drawn_counts = jax.random.randint(base_key, (partitions,), PAIR // 2, PAIR + 1, dtype=jnp.int32)
    chosen = jax.random.randint(pick_key, (), 0, partitions, dtype=jnp.int32)
    drawn_counts = jnp.where(jnp.arange(partitions, dtype=jnp.int32) == chosen, PAIR, drawn_counts)
    return drawn_counts.reshape(N_DOM, N_GRP)


def draw_counts(key, part):
    return pair_counts(key)


def draw_elem_faces(key, part):
    counts = pair_counts(key)
    key = jax.random.fold_in(key, 5)
    second_key, shuffle_key = jax.random.split(key)
    partitions = N_DOM * N_GRP
    lower_counts = jnp.roll(counts, 1, axis=0)
    second_count = 4 * ELEMS - INNER - counts - lower_counts
    second_ids = jax.vmap(lambda k: jax.random.permutation(k, INNER))(jax.random.split(second_key, partitions))
    second_ids = second_ids.reshape(N_DOM, N_GRP, INNER).astype(jnp.int32)
    inner_range = jnp.arange(INNER, dtype=jnp.int32)
    slot_range = jnp.arange(PAIR, dtype=jnp.int32)
    shape_head = (N_DOM, N_GRP)
    slot_ids = jnp.concatenate([jnp.broadcast_to(inner_range, shape_head + (INNER,)), second_ids, jnp.broadcast_to(INNER + slot_range, shape_head + (PAIR,)), jnp.broadcast_to(INNER + PAIR + slot_range, shape_head + (PAIR,))], axis=-1)
    is_valid = jnp.concatenate([jnp.ones(shape_head + (INNER,), jnp.int32), (inner_range < second_count[..., None]).astype(jnp.int32), (slot_range < counts[..., None]).astype(jnp.int32), (slot_range < lower_counts[..., None]).astype(jnp.int32)], axis=-1)
    candidates = 2 * INNER + 2 * PAIR
    shuffle_rank = jax.vmap(lambda k: jax.random.permutation(k, candidates))(jax.random.split(shuffle_key, partitions))
    shuffle_rank = shuffle_rank.reshape(N_DOM, N_GRP, candidates).astype(jnp.int32)
    sort_key = (1 - is_valid) * candidates + shuffle_rank
    ordering = jnp.argsort(sort_key, axis=-1)
    chosen = jnp.take_along_axis(slot_ids, ordering[..., :4 * ELEMS], axis=-1)
    return chosen.reshape(N_DOM, N_GRP, ELEMS, 4).astype(jnp.int32)


def touch_ends(entries, key, low, top_value):
    shape = entries.shape
    index_at = [jax.random.randint(jax.random.fold_in(key, axis), (), 0, shape[axis]) for axis in range(len(shape))]
    entries = entries.at[tuple(index_at)].set(low)
    longest = shape.index(max(shape))
    index_at[longest] = (index_at[longest] + 1) % shape[longest]
    return entries.at[tuple(index_at)].set(top_value)


def shard_levels(rng, shape, shards, smallest, top_value):
    level = 1.0
    for dim, blocks in shards:
        draws = jax.random.uniform(jax.random.fold_in(jax.random.fold_in(rng, 6), dim), (blocks,), jnp.float32, smallest / len(shards), top_value / len(shards))
        level = level * jnp.repeat(jnp.exp(draws), shape[dim] // blocks).reshape((-1,) + (1,) * (len(shape) - 1 - dim))
    return level


def gaussian(key, shape, deviation, reach, cuts=(), kind=jnp.bfloat16):
    drawn = deviation * jax.random.normal(key, shape, jnp.float32)
    if cuts:
        drawn = drawn * shard_levels(key, shape, cuts, -0.22, 0.18)
    return jnp.clip(drawn, -reach, reach).astype(kind)


def setup_inputs(seed: int = 0) -> dict:
    key_list = jax.random.split(jax.random.key(seed), 7)
    trace = gaussian(key_list[0], (N_DOM, N_GRP, F_OWN, ROW), 1.0, 6.0, ((0, 192), (1, 4)), jnp.float32)
    rhs = gaussian(key_list[1], (N_DOM, N_GRP, F_OWN, ROW), 1.0, 6.0, ((0, 192), (1, 4)), jnp.float32)
    stiffness = gaussian(key_list[2], (N_DOM, N_GRP, ELEMS, TRACE * TRACE), TRACE ** -0.5, 0.5, ((0, 192), (1, 4)), jnp.float32)
    elem_faces = draw_elem_faces(jax.random.fold_in(key_list[6], 71), 0)
    orient = touch_ends(jax.random.randint(key_list[4], (N_DOM, N_GRP, ELEMS, 4), 0, 6), jax.random.fold_in(key_list[4], 1), 0, 5).astype(jnp.int32)
    counts = draw_counts(jax.random.fold_in(key_list[6], 71), 0)
    return dict(trace=trace, rhs=rhs, stiffness=stiffness, elem_faces=elem_faces, orient=orient, counts=counts)


def face_tables():
    node_list = [(a, b, 3 - a - b) for a in range(4) for b in range(4 - a)]
    orderings = [(0, 1, 2), (1, 2, 0), (2, 0, 1), (0, 2, 1), (2, 1, 0), (1, 0, 2)]
    node_table = np.zeros((6, 10, 10), np.float32)
    for orient_id, ordering in enumerate(orderings):
        for node_id, coords in enumerate(node_list):
            target = node_list.index((coords[ordering[0]], coords[ordering[1]], coords[ordering[2]]))
            node_table[orient_id, node_id, target] = 1.0
    barycentric = np.array(node_list, np.float32) / 3.0
    return node_table, barycentric


def apply_elements(local_trace, stiffness, elem_faces, orient):
    node_table, barycentric = face_tables()
    elements = stiffness.shape[0]
    row_width = local_trace.shape[1] // NODES
    matrices = stiffness.reshape(elements, TRACE, TRACE)
    picked = local_trace[elem_faces].reshape(elements, 4, NODES, row_width)
    onehot = (orient[..., None] == jnp.arange(6, dtype=jnp.int32)).astype(local_trace.dtype)
    selector = jnp.einsum("efo,onm->efnm", onehot, jnp.asarray(node_table, local_trace.dtype), precision=lax.Precision.HIGHEST)
    values = jnp.einsum("efnm,efmc->efnc", selector, picked, precision=lax.Precision.HIGHEST)
    values = values.reshape(elements, TRACE, -1)
    result = jnp.einsum("eij,ejr->eir", matrices, values, precision=lax.Precision.HIGHEST)
    result = result.reshape(elements, 4, NODES, row_width)
    returned = jnp.einsum("efnm,efnc->efmc", selector, result, precision=lax.Precision.HIGHEST)
    returned = returned.reshape(elements * 4, NODES * row_width)
    return jax.ops.segment_sum(returned, elem_faces.reshape(-1), num_segments=local_trace.shape[0])


def reference(trace, rhs, stiffness, elem_faces, orient, counts):
    node_table, barycentric = face_tables()
    owned_shared = trace[:, :, INNER:]
    from_below = jnp.concatenate([jnp.zeros_like(owned_shared[:1]), owned_shared[:-1]], axis=0)
    local_trace = jnp.concatenate([trace, from_below], axis=2)

    def one_partition(partition):
        return jax.vmap(apply_elements)(*partition)

    partial_value = lax.map(one_partition, (local_trace, stiffness, elem_faces, orient))
    interior = partial_value[:, :, :INNER]
    part_owned = partial_value[:, :, INNER:F_OWN]
    part_lower = partial_value[:, :, F_OWN:]
    from_above = jnp.concatenate([part_lower[1:], jnp.zeros_like(part_lower[:1])], axis=0)
    from_beneath = jnp.concatenate([jnp.zeros_like(part_owned[:1]), part_owned[:-1]], axis=0)
    condensed = jnp.concatenate([interior, part_owned + from_above, part_lower + from_beneath], axis=2)
    residual = rhs - condensed[:, :, :F_OWN]
    row_index = jnp.arange(F_OWN, dtype=jnp.int32)
    keep_rows = row_index[None, None, :] < INNER + counts[:, :, None]
    residual = jnp.where(keep_rows[..., None], residual, jnp.zeros_like(residual))
    residual = residual.reshape(N_DOM, N_GRP, F_OWN, NODES, FIELDS * RHS)
    coarse = jnp.einsum("nv,dgfnc->dgfvc", jnp.asarray(barycentric, residual.dtype), residual, precision=lax.Precision.HIGHEST)
    coarse = coarse.reshape(N_DOM, N_GRP * F_OWN, VERTS * FIELDS * RHS)
    return condensed, coarse
```

```python
import jax
import jax.numpy as jnp
import numpy as np
from jax import lax
from jax.experimental import pallas as pl
from jax.experimental.pallas import tpu as pltpu
from jax.sharding import PartitionSpec as P

F32 = jnp.float32
BF16 = jnp.bfloat16
MESH = pl.DeviceIdType.MESH
ELEMS = 32
NODES = 10
INNER = 64
OWN = 72
SLOTS = 80
ROW = 1280
COARSE = 384
HEAD = 40

NODE_LIST = [(a, b, 3 - a - b) for a in range(4) for b in range(4 - a)]
ORDERINGS = [(0, 1, 2), (1, 2, 0), (2, 0, 1), (0, 2, 1), (2, 1, 0), (1, 0, 2)]
PERM = [
    [NODE_LIST.index((c[p[0]], c[p[1]], c[p[2]])) for c in NODE_LIST] for p in ORDERINGS
]
INVERSE = [[row.index(m) for m in range(NODES)] for row in PERM]
BARY = np.array(NODE_LIST, np.float32) / np.float32(3.0)


def split(x):
    high = x.astype(BF16)
    return high, (x - high.astype(F32)).astype(BF16)


def dot(a, b):
    return jnp.dot(a, b, preferred_element_type=F32)


def iota(shape, dim):
    return lax.broadcasted_iota(jnp.int32, shape, dim)


def spread(small):
    pick = (iota((128, 4), 0) % 4 == iota((128, 4), 1)).astype(F32).astype(BF16)
    rows = dot(pick, small.astype(F32).astype(BF16))
    rows = jnp.where(iota((128, ELEMS), 0) // 4 == iota((128, ELEMS), 1), rows, 0.0)
    return dot(rows.astype(BF16), jnp.ones((ELEMS, 128), BF16))


def oriented(orient, slabs, table, node):
    if all(table[o][node] == node for o in range(6)):
        return slabs[node]
    out = slabs[table[5][node]]
    for o in range(4, -1, -1):
        out = jnp.where(orient == o, slabs[table[o][node]], out)
    return out


def build_selectors(faces_ref, orient_ref, pick_ref, back_ref, turn_ref):
    faces = spread(faces_ref[...])
    turn_ref[...] = spread(orient_ref[...])
    pick = (faces == iota((128, 128), 1).astype(F32)).astype(F32)
    pick_ref[:, :128] = pick.astype(BF16)
    pick_ref[:, 128:] = pick.astype(BF16)
    back = pick.T.astype(BF16)
    back_ref[:, :128] = back
    back_ref[:, 128:] = back


def gather_values(local_ref, pick_ref, turn_ref, pieces_ref, values_ref):
    high, low = split(local_ref[...])
    nothing = jnp.zeros((128 - SLOTS, ROW), BF16)
    pieces_ref[0:80, :] = high
    pieces_ref[80:128, :] = nothing
    pieces_ref[128:208, :] = low
    pieces_ref[208:256, :] = nothing
    pick = pick_ref[...]
    slabs = []
    for pair in range(NODES // 2):
        both = dot(pick, pieces_ref[:, pair * 256 : (pair + 1) * 256])
        slabs += [both[:, :128], both[:, 128:]]
    turn = turn_ref[...]
    group = iota((128, 128), 1) // 32
    for node in range(NODES):
        value = oriented(turn, slabs, PERM, node)
        moved = [value] + [pltpu.roll(value, 32 * s, 1) for s in (1, 2, 3)]
        for field in range(4):
            out = moved[(3 - field) % 4]
            for g in (2, 1, 0):
                out = jnp.where(group == g, moved[(g - field) % 4], out)
            values_ref[pl.ds(node * 4 + field, 128, stride=40), :] = out


def element_product(e, matrix_ref, values_ref, result_ref):
    values = values_ref[pl.ds(e * 160, 160), :]
    lane = iota((40, 128), 1)
    group = lane // 32
    high, low = split(values[:128])
    main = jnp.concatenate([high, low], axis=1)
    main = jnp.concatenate([main, main], axis=0)
    last = values[128:160]
    group32 = iota((32, 128), 1) // 32
    rest = jnp.concatenate([jnp.where(group32 == b, last, 0.0) for b in range(4)], axis=0)
    high, low = split(rest)
    rest = jnp.concatenate([high, low], axis=1)
    rest = jnp.concatenate([rest, rest], axis=0)
    parts = [matrix_ref[e, pl.ds(c, 40, stride=5), :] for c in range(5)]
    rows = [parts[0]]
    for b in range(1, 4):
        mixed = jnp.where(lane >= 32 * b, parts[b], parts[b + 1])
        rows.append(pltpu.roll(mixed, 128 - 32 * b, 1))
    high, low = split(jnp.concatenate(rows, axis=0))
    first = dot(jnp.concatenate([high, low], axis=1), main)
    tail = jnp.where(
        group == 0, parts[1], jnp.where(group == 1, parts[2], jnp.where(group == 2, parts[3], parts[4]))
    )
    high, low = split(tail)
    second = dot(jnp.concatenate([high, low], axis=1), rest)
    first = first[:, :128] + first[:, 128:]
    second = second[:, :128] + second[:, 128:]
    out = jnp.where(
        group == 0,
        first[0:40],
        jnp.where(group == 1, first[40:80], jnp.where(group == 2, first[80:120], first[120:160])),
    )
    result_ref[pl.ds(e * 40, 40), :] = out + second


def scatter_results(result_ref, back_ref, turn_ref, partial_ref):
    turn = turn_ref[...]
    slabs = [result_ref[pl.ds(n, 128, stride=NODES), :] for n in range(NODES)]
    back = back_ref[0:SLOTS, :]
    for pair in range(NODES // 2):
        both = [oriented(turn, slabs, INVERSE, m) for m in (2 * pair, 2 * pair + 1)]
        high, low = split(jnp.concatenate(both, axis=1))
        partial_ref[:, pair * 256 : (pair + 1) * 256] = dot(back, jnp.concatenate([high, low], axis=0))


def project(rows):
    out = []
    for v in range(3):
        terms = [float(BARY[n, v]) * rows(n) for n in range(NODES) if BARY[n, v] != 0]
        total = terms[0]
        for term in terms[1:]:
            total = total + term
        out.append(total)
    return out


def kernel(
    n_dom,
    trace_hbm,
    rhs_hbm,
    matrix_hbm,
    faces_hbm,
    orient_hbm,
    counts_hbm,
    cond_ref,
    coarse_ref,
    local,
    rhs,
    matrix,
    faces,
    orient,
    counts,
    pick,
    back,
    turn,
    pieces,
    values,
    result,
    shared,
    arrived,
    low_out,
    low_in,
    in_sem,
    matrix_sem,
    dom_send,
    dom_recv,
    low_send,
    low_recv,
    grp_send,
    grp_recv,
):
    d = lax.axis_index("dom")
    g = lax.axis_index("grp")
    has_below = d > 0
    has_above = d < n_dom - 1
    right = lax.rem(g + 1, 4)
    left = lax.rem(g + 3, 4)
    opposite = lax.rem(g + 2, 4)

    loads = [
        pltpu.make_async_copy(trace_hbm, local.at[pl.ds(0, OWN)], in_sem.at[0]),
        pltpu.make_async_copy(faces_hbm, faces, in_sem.at[1]),
        pltpu.make_async_copy(orient_hbm, orient, in_sem.at[2]),
        pltpu.make_async_copy(counts_hbm, counts, in_sem.at[3]),
        pltpu.make_async_copy(rhs_hbm, rhs, in_sem.at[4]),
    ]
    for load in loads[:4]:
        load.start()

    barrier = pltpu.get_barrier_semaphore()

    def greet(dom, grp):
        pl.semaphore_signal(barrier, inc=1, device_id=(dom, grp), device_id_type=MESH)

    greet(d, right)
    greet(d, left)

    @pl.when(has_below)
    def _():
        greet(d - 1, g)

    @pl.when(has_above)
    def _():
        for i in range(4):
            greet(d + 1, lax.rem(g + i, 4))

    matrix_loads = [
        pltpu.make_async_copy(matrix_hbm.at[e // 8, :, e % 8, :], matrix.at[e], matrix_sem.at[e])
        for e in range(ELEMS)
    ]
    for load in matrix_loads:
        load.start()
    loads[4].start()

    pl.semaphore_wait(barrier, 2 + 4 * has_below.astype(jnp.int32) + has_above.astype(jnp.int32))

    def remote(src, dst, send, recv, dom, grp):
        return pltpu.make_async_remote_copy(
            src_ref=src,
            dst_ref=dst,
            send_sem=send,
            recv_sem=recv,
            device_id=(dom, grp),
            device_id_type=MESH,
        )

    trace_up = remote(
        trace_hbm.at[pl.ds(INNER, 8)], local.at[pl.ds(OWN, 8)], dom_send.at[0], dom_recv.at[0], d + 1, g
    )
    part_up = remote(shared.at[0], arrived.at[0], dom_send.at[1], dom_recv.at[1], d + 1, g)
    part_down = remote(shared.at[1], arrived.at[1], dom_send.at[2], dom_recv.at[2], d - 1, g)
    low_down = [
        remote(low_out, low_in.at[i], low_send.at[i], low_recv.at[i], d - 1, lax.rem(g + i, 4))
        for i in range(4)
    ]

    @pl.when(has_above)
    def _():
        trace_up.start()

    @pl.when(jnp.logical_not(has_below))
    def _():
        local[OWN:SLOTS, :] = jnp.zeros((8, ROW), F32)

    loads[1].wait()
    loads[2].wait()
    build_selectors(faces, orient, pick, back, turn)
    loads[0].wait()

    @pl.when(has_below)
    def _():
        trace_up.wait_recv()

    gather_values(local, pick, turn, pieces, values)
    for load in matrix_loads:
        load.wait()

    def step(e, carry):
        element_product(e, matrix, values, result)
        return carry

    lax.fori_loop(0, ELEMS, step, 0, unroll=8)
    scatter_results(result, back, turn, cond_ref)

    shared[0] = cond_ref[INNER:OWN, :]
    shared[1] = cond_ref[OWN:SLOTS, :]
    low = project(lambda n: cond_ref[OWN:SLOTS, n * 128 : (n + 1) * 128])
    for v in range(3):
        low_out[:, v * 128 : (v + 1) * 128] = low[v]

    @pl.when(has_below)
    def _():
        part_down.start()
        for copy in low_down:
            copy.start()

    @pl.when(has_above)
    def _():
        part_up.start()

    loads[3].wait()
    loads[4].wait()
    mine = pl.multiple_of(g * OWN, 8)
    own = project(
        lambda n: rhs[:, n * 128 : (n + 1) * 128] - cond_ref[0:OWN, n * 128 : (n + 1) * 128]
    )
    keep = iota((OWN, 128), 0) < INNER + counts[...]
    for v in range(3):
        coarse_ref[pl.ds(mine, OWN), v * 128 : (v + 1) * 128] = jnp.where(keep, own[v], 0.0)

    def piece(owner, which):
        start = pl.multiple_of(owner * OWN + HEAD * which, 8)
        return coarse_ref.at[pl.ds(start, (HEAD, OWN - HEAD)[which])]

    def pass_on(owner, which, number, to):
        return remote(
            piece(owner, which),
            piece(owner, which),
            grp_send.at[number],
            grp_recv.at[number],
            d,
            to,
        )

    sends = [
        pass_on(g, 0, 0, right),
        pass_on(g, 1, 1, left),
        pass_on(g, 1, 2, right),
        pass_on(g, 0, 3, left),
    ]
    for copy in sends:
        copy.start()
    onward = [pass_on(left, 0, 4, right), pass_on(right, 1, 5, left)]

    def arrival(owner, which, number):
        return remote(
            piece(owner, which),
            piece(owner, which),
            grp_send.at[number],
            grp_recv.at[number],
            d,
            right,
        )

    arrival(left, 0, 0).wait_recv()
    onward[0].start()
    arrival(right, 1, 1).wait_recv()
    onward[1].start()

    @pl.when(has_above)
    def _():
        part_down.wait_recv()
        cond_ref[INNER:OWN, :] = shared[0] + arrived[1]

    @pl.when(has_below)
    def _():
        part_up.wait_recv()
        cond_ref[OWN:SLOTS, :] = shared[1] + arrived[0]

    arrival(left, 1, 2).wait_recv()
    arrival(right, 0, 3).wait_recv()
    for copy in sends:
        copy.wait_send()
    for copy in onward:
        copy.wait_send()
    arrival(opposite, 0, 4).wait_recv()
    arrival(opposite, 1, 5).wait_recv()

    @pl.when(has_above)
    def _():
        for i in range(4):
            low_down[i].wait_recv()
            owner = lax.rem(g + 4 - i, 4)
            rows = pl.ds(pl.multiple_of(owner * OWN + INNER, 8), 8)
            coarse_ref[rows, :] = coarse_ref[rows, :] - low_in[i]

    @pl.when(has_above)
    def _():
        trace_up.wait_send()
        part_up.wait_send()

    @pl.when(has_below)
    def _():
        part_down.wait_send()
        for copy in low_down:
            copy.wait_send()


def body(trace, rhs, stiffness, elem_faces, orient, counts):
    n_dom = lax.axis_size("dom")
    matrix = stiffness.reshape(4, 8, 200, 128).transpose(0, 2, 1, 3)
    hbm = pl.BlockSpec(memory_space=pl.ANY)
    vmem = pl.BlockSpec(memory_space=pltpu.VMEM)
    dma = pltpu.SemaphoreType.DMA
    cond, coarse = pl.pallas_call(
        lambda *refs: kernel(n_dom, *refs),
        out_shape=(
            jax.ShapeDtypeStruct((SLOTS, ROW), F32),
            jax.ShapeDtypeStruct((4 * OWN, COARSE), F32),
        ),
        in_specs=[hbm] * 6,
        out_specs=(vmem, vmem),
        scratch_shapes=[
            pltpu.VMEM((SLOTS, ROW), F32),
            pltpu.VMEM((OWN, ROW), F32),
            pltpu.VMEM((ELEMS, 200, 128), F32),
            pltpu.VMEM((4, ELEMS), jnp.int32),
            pltpu.VMEM((4, ELEMS), jnp.int32),
            pltpu.VMEM((1, 1), jnp.int32),
            pltpu.VMEM((128, 256), BF16),
            pltpu.VMEM((128, 256), BF16),
            pltpu.VMEM((128, 128), F32),
            pltpu.VMEM((256, ROW), BF16),
            pltpu.VMEM((ELEMS * 160, 128), F32),
            pltpu.VMEM((ELEMS * 40, 128), F32),
            pltpu.VMEM((2, 8, ROW), F32),
            pltpu.VMEM((2, 8, ROW), F32),
            pltpu.VMEM((8, COARSE), F32),
            pltpu.VMEM((4, 8, COARSE), F32),
            dma((5,)),
            dma((ELEMS,)),
            dma((3,)),
            dma((3,)),
            dma((4,)),
            dma((4,)),
            dma((6,)),
            dma((6,)),
        ],
        compiler_params=pltpu.CompilerParams(
            collective_id=0, has_side_effects=True, vmem_limit_bytes=60 * 2**20
        ),
    )(
        trace[0, 0],
        rhs[0, 0],
        matrix,
        elem_faces[0, 0].T,
        orient[0, 0].T,
        counts,
    )
    return cond[None, None], coarse[None]


def solution(mesh):
    part = P("dom", "grp", None, None)
    return jax.shard_map(
        body,
        mesh=mesh,
        in_specs=(part, part, part, part, part, P("dom", "grp")),
        out_specs=(part, P("dom", None, None)),
        check_vma=False,
    )
```

```python
import jax
import jax.numpy as jnp
import numpy as np
from jax import lax
from jax.experimental import pallas as pl
from jax.experimental.pallas import tpu as pltpu
from jax.sharding import PartitionSpec as P

F32 = jnp.float32
BF16 = jnp.bfloat16
MESH = pl.DeviceIdType.MESH
ELEMS = 32
NODES = 10
INNER = 64
OWN = 72
SLOTS = 80
ROW = 1280
COARSE = 384
HEAD = 40

NODE_LIST = [(a, b, 3 - a - b) for a in range(4) for b in range(4 - a)]
ORDERINGS = [(0, 1, 2), (1, 2, 0), (2, 0, 1), (0, 2, 1), (2, 1, 0), (1, 0, 2)]
PERM = [
    [NODE_LIST.index((c[p[0]], c[p[1]], c[p[2]])) for c in NODE_LIST] for p in ORDERINGS
]
INVERSE = [[row.index(m) for m in range(NODES)] for row in PERM]
BARY = np.array(NODE_LIST, np.float32) / np.float32(3.0)


def split(x):
    high = x.astype(BF16)
    return high, (x - high.astype(F32)).astype(BF16)


def dot(a, b):
    return jnp.dot(a, b, preferred_element_type=F32)


def iota(shape, dim):
    return lax.broadcasted_iota(jnp.int32, shape, dim)


def spread(small):
    pick = (iota((128, 4), 0) % 4 == iota((128, 4), 1)).astype(F32).astype(BF16)
    rows = dot(pick, small.astype(F32).astype(BF16))
    rows = jnp.where(iota((128, ELEMS), 0) // 4 == iota((128, ELEMS), 1), rows, 0.0)
    return dot(rows.astype(BF16), jnp.ones((ELEMS, 128), BF16))


def oriented(orient, slabs, table, node):
    if all(table[o][node] == node for o in range(6)):
        return slabs[node]
    out = slabs[table[5][node]]
    for o in range(4, -1, -1):
        out = jnp.where(orient == o, slabs[table[o][node]], out)
    return out


def build_selectors(faces_ref, orient_ref, pick_ref, back_ref, turn_ref):
    faces = spread(faces_ref[...])
    turn_ref[...] = spread(orient_ref[...])
    pick = (faces == iota((128, 128), 1).astype(F32)).astype(F32)
    pick_ref[:, :128] = pick.astype(BF16)
    pick_ref[:, 128:] = pick.astype(BF16)
    back = pick.T.astype(BF16)
    back_ref[:, :128] = back
    back_ref[:, 128:] = back


def gather_values(local_ref, pick_ref, turn_ref, pieces_ref, values_ref):
    high, low = split(local_ref[...])
    nothing = jnp.zeros((128 - SLOTS, ROW), BF16)
    pieces_ref[0:80, :] = high
    pieces_ref[80:128, :] = nothing
    pieces_ref[128:208, :] = low
    pieces_ref[208:256, :] = nothing
    pick = pick_ref[...]
    slabs = []
    for pair in range(NODES // 2):
        both = dot(pick, pieces_ref[:, pair * 256 : (pair + 1) * 256])
        slabs += [both[:, :128], both[:, 128:]]
    turn = turn_ref[...]
    group = iota((128, 128), 1) // 32
    for node in range(NODES):
        value = oriented(turn, slabs, PERM, node)
        moved = [value] + [pltpu.roll(value, 32 * s, 1) for s in (1, 2, 3)]
        for field in range(4):
            out = moved[(3 - field) % 4]
            for g in (2, 1, 0):
                out = jnp.where(group == g, moved[(g - field) % 4], out)
            values_ref[pl.ds(node * 4 + field, 128, stride=40), :] = out


def element_product(e, matrix_ref, values_ref, result_ref):
    values = values_ref[pl.ds(e * 160, 160), :]
    lane = iota((40, 128), 1)
    group = lane // 32
    high, low = split(values[:128])
    main = jnp.concatenate([high, low], axis=1)
    main = jnp.concatenate([main, main], axis=0)
    last = values[128:160]
    group32 = iota((32, 128), 1) // 32
    rest = jnp.concatenate([jnp.where(group32 == b, last, 0.0) for b in range(4)], axis=0)
    high, low = split(rest)
    rest = jnp.concatenate([high, low], axis=1)
    rest = jnp.concatenate([rest, rest], axis=0)
    parts = [matrix_ref[e, pl.ds(c, 40, stride=5), :] for c in range(5)]
    rows = [parts[0]]
    for b in range(1, 4):
        mixed = jnp.where(lane >= 32 * b, parts[b], parts[b + 1])
        rows.append(pltpu.roll(mixed, 128 - 32 * b, 1))
    high, low = split(jnp.concatenate(rows, axis=0))
    first = dot(jnp.concatenate([high, low], axis=1), main)
    tail = jnp.where(
        group == 0, parts[1], jnp.where(group == 1, parts[2], jnp.where(group == 2, parts[3], parts[4]))
    )
    high, low = split(tail)
    second = dot(jnp.concatenate([high, low], axis=1), rest)
    first = first[:, :128] + first[:, 128:]
    second = second[:, :128] + second[:, 128:]
    out = jnp.where(
        group == 0,
        first[0:40],
        jnp.where(group == 1, first[40:80], jnp.where(group == 2, first[80:120], first[120:160])),
    )
    result_ref[pl.ds(e * 40, 40), :] = out + second


def scatter_results(result_ref, back_ref, turn_ref, partial_ref):
    turn = turn_ref[...]
    slabs = [result_ref[pl.ds(n, 128, stride=NODES), :] for n in range(NODES)]
    back = back_ref[0:SLOTS, :]
    for pair in range(NODES // 2):
        both = [oriented(turn, slabs, INVERSE, m) for m in (2 * pair, 2 * pair + 1)]
        high, low = split(jnp.concatenate(both, axis=1))
        partial_ref[:, pair * 256 : (pair + 1) * 256] = dot(back, jnp.concatenate([high, low], axis=0))


def project(rows):
    out = []
    for v in range(3):
        terms = [float(BARY[n, v]) * rows(n) for n in range(NODES) if BARY[n, v] != 0]
        total = terms[0]
        for term in terms[1:]:
            total = total + term
        out.append(total)
    return out


def kernel(
    n_dom,
    trace_hbm,
    rhs_hbm,
    matrix_hbm,
    faces_hbm,
    orient_hbm,
    cond_ref,
    coarse_ref,
    local,
    rhs,
    matrix,
    faces,
    orient,
    pick,
    back,
    turn,
    pieces,
    values,
    result,
    shared,
    arrived,
    low_out,
    low_in,
    in_sem,
    matrix_sem,
    dom_send,
    dom_recv,
    low_send,
    low_recv,
    grp_send,
    grp_recv,
):
    d = lax.axis_index("dom")
    g = lax.axis_index("grp")
    has_below = d > 0
    has_above = d < n_dom - 1
    right = lax.rem(g + 1, 4)
    left = lax.rem(g + 3, 4)
    opposite = lax.rem(g + 2, 4)

    loads = [
        pltpu.make_async_copy(trace_hbm, local.at[pl.ds(0, OWN)], in_sem.at[0]),
        pltpu.make_async_copy(faces_hbm, faces, in_sem.at[1]),
        pltpu.make_async_copy(orient_hbm, orient, in_sem.at[2]),
        pltpu.make_async_copy(rhs_hbm, rhs, in_sem.at[3]),
    ]
    for load in loads[:3]:
        load.start()

    barrier = pltpu.get_barrier_semaphore()

    def greet(dom, grp):
        pl.semaphore_signal(barrier, inc=1, device_id=(dom, grp), device_id_type=MESH)

    greet(d, right)
    greet(d, left)

    @pl.when(has_below)
    def _():
        greet(d - 1, g)

    @pl.when(has_above)
    def _():
        for i in range(4):
            greet(d + 1, lax.rem(g + i, 4))

    matrix_loads = [
        pltpu.make_async_copy(matrix_hbm.at[e // 8, :, e % 8, :], matrix.at[e], matrix_sem.at[e])
        for e in range(ELEMS)
    ]
    for load in matrix_loads:
        load.start()
    loads[3].start()

    pl.semaphore_wait(barrier, 2 + 4 * has_below.astype(jnp.int32) + has_above.astype(jnp.int32))

    def remote(src, dst, send, recv, dom, grp):
        return pltpu.make_async_remote_copy(
            src_ref=src,
            dst_ref=dst,
            send_sem=send,
            recv_sem=recv,
            device_id=(dom, grp),
            device_id_type=MESH,
        )

    trace_up = remote(
        trace_hbm.at[pl.ds(INNER, 8)], local.at[pl.ds(OWN, 8)], dom_send.at[0], dom_recv.at[0], d + 1, g
    )
    part_up = remote(shared.at[0], arrived.at[0], dom_send.at[1], dom_recv.at[1], d + 1, g)
    part_down = remote(shared.at[1], arrived.at[1], dom_send.at[2], dom_recv.at[2], d - 1, g)
    low_down = [
        remote(low_out, low_in.at[i], low_send.at[i], low_recv.at[i], d - 1, lax.rem(g + i, 4))
        for i in range(4)
    ]

    @pl.when(has_above)
    def _():
        trace_up.start()

    @pl.when(jnp.logical_not(has_below))
    def _():
        local[OWN:SLOTS, :] = jnp.zeros((8, ROW), F32)

    loads[1].wait()
    loads[2].wait()
    build_selectors(faces, orient, pick, back, turn)
    loads[0].wait()

    @pl.when(has_below)
    def _():
        trace_up.wait_recv()

    gather_values(local, pick, turn, pieces, values)

    def block(i, carry):
        for q in range(8):
            e = i * 8 + q
            pltpu.make_async_copy(matrix_hbm.at[0, :, 0, :], matrix.at[e], matrix_sem.at[e]).wait()
        for q in range(8):
            element_product(i * 8 + q, matrix, values, result)
        return carry

    lax.fori_loop(0, ELEMS // 8, block, 0)
    scatter_results(result, back, turn, cond_ref)

    shared[0] = cond_ref[INNER:OWN, :]
    shared[1] = cond_ref[OWN:SLOTS, :]
    low = project(lambda n: cond_ref[OWN:SLOTS, n * 128 : (n + 1) * 128])
    for v in range(3):
        low_out[:, v * 128 : (v + 1) * 128] = low[v]

    @pl.when(has_below)
    def _():
        part_down.start()
        for copy in low_down:
            copy.start()

    @pl.when(has_above)
    def _():
        part_up.start()

    loads[3].wait()
    mine = pl.multiple_of(g * OWN, 8)
    own = project(
        lambda n: rhs[:, n * 128 : (n + 1) * 128] - cond_ref[0:OWN, n * 128 : (n + 1) * 128]
    )
    named = dot(back[0:SLOTS, :128], jnp.ones((128, 128), BF16))[:OWN]
    keep = jnp.logical_or(iota((OWN, 128), 0) < INNER, named > 0.5)
    for v in range(3):
        coarse_ref[pl.ds(mine, OWN), v * 128 : (v + 1) * 128] = jnp.where(keep, own[v], 0.0)

    def piece(owner, which):
        start = pl.multiple_of(owner * OWN + HEAD * which, 8)
        return coarse_ref.at[pl.ds(start, (HEAD, OWN - HEAD)[which])]

    def pass_on(owner, which, number, to):
        return remote(
            piece(owner, which),
            piece(owner, which),
            grp_send.at[number],
            grp_recv.at[number],
            d,
            to,
        )

    sends = [
        pass_on(g, 0, 0, right),
        pass_on(g, 1, 1, left),
        pass_on(g, 1, 2, right),
        pass_on(g, 0, 3, left),
    ]
    for copy in sends:
        copy.start()
    onward = [pass_on(left, 0, 4, right), pass_on(right, 1, 5, left)]

    def arrival(owner, which, number):
        return remote(
            piece(owner, which),
            piece(owner, which),
            grp_send.at[number],
            grp_recv.at[number],
            d,
            right,
        )

    arrival(left, 0, 0).wait_recv()
    onward[0].start()
    arrival(right, 1, 1).wait_recv()
    onward[1].start()

    @pl.when(has_above)
    def _():
        part_down.wait_recv()
        cond_ref[INNER:OWN, :] = shared[0] + arrived[1]

    @pl.when(has_below)
    def _():
        part_up.wait_recv()
        cond_ref[OWN:SLOTS, :] = shared[1] + arrived[0]

    arrival(left, 1, 2).wait_recv()
    arrival(right, 0, 3).wait_recv()
    for copy in sends:
        copy.wait_send()
    for copy in onward:
        copy.wait_send()
    arrival(opposite, 0, 4).wait_recv()
    arrival(opposite, 1, 5).wait_recv()

    @pl.when(has_above)
    def _():
        for i in range(4):
            low_down[i].wait_recv()
            owner = lax.rem(g + 4 - i, 4)
            rows = pl.ds(pl.multiple_of(owner * OWN + INNER, 8), 8)
            coarse_ref[rows, :] = coarse_ref[rows, :] - low_in[i]

    @pl.when(has_above)
    def _():
        trace_up.wait_send()
        part_up.wait_send()

    @pl.when(has_below)
    def _():
        part_down.wait_send()
        for copy in low_down:
            copy.wait_send()


def write_out(cond, coarse, cond_out, coarse_out, sem):
    copies = []
    for half in range(2):
        rows = pl.ds(half * 40, 40)
        copies.append(pltpu.make_async_copy(cond.at[rows], cond_out.at[rows], sem.at[half]))
        rows = pl.ds(half * 144, 144)
        copies.append(pltpu.make_async_copy(coarse.at[rows], coarse_out.at[rows], sem.at[2 + half]))
    for copy in copies:
        copy.start()
    for copy in copies:
        copy.wait()


def body(trace, rhs, stiffness, elem_faces, orient, counts):
    n_dom = lax.axis_size("dom")
    matrix = stiffness.reshape(4, 8, 200, 128).transpose(0, 2, 1, 3)
    hbm = pl.BlockSpec(memory_space=pl.ANY)
    vmem = pl.BlockSpec(memory_space=pltpu.VMEM)
    dma = pltpu.SemaphoreType.DMA
    cond, coarse = pl.pallas_call(
        lambda *refs: kernel(n_dom, *refs),
        out_shape=(
            pltpu.VMEM((SLOTS, ROW), F32),
            pltpu.VMEM((4 * OWN, COARSE), F32),
        ),
        in_specs=[hbm] * 5,
        out_specs=(vmem, vmem),
        scratch_shapes=[
            pltpu.VMEM((SLOTS, ROW), F32),
            pltpu.VMEM((OWN, ROW), F32),
            pltpu.VMEM((ELEMS, 200, 128), F32),
            pltpu.VMEM((4, ELEMS), jnp.int32),
            pltpu.VMEM((4, ELEMS), jnp.int32),
            pltpu.VMEM((128, 256), BF16),
            pltpu.VMEM((128, 256), BF16),
            pltpu.VMEM((128, 128), F32),
            pltpu.VMEM((256, ROW), BF16),
            pltpu.VMEM((ELEMS * 160, 128), F32),
            pltpu.VMEM((ELEMS * 40, 128), F32),
            pltpu.VMEM((2, 8, ROW), F32),
            pltpu.VMEM((2, 8, ROW), F32),
            pltpu.VMEM((8, COARSE), F32),
            pltpu.VMEM((4, 8, COARSE), F32),
            dma((4,)),
            dma((ELEMS,)),
            dma((3,)),
            dma((3,)),
            dma((4,)),
            dma((4,)),
            dma((6,)),
            dma((6,)),
        ],
        compiler_params=pltpu.CompilerParams(
            collective_id=0, has_side_effects=True, vmem_limit_bytes=62_488_000
        ),
    )(
        trace[0, 0],
        rhs[0, 0],
        matrix,
        elem_faces[0, 0].T,
        orient[0, 0].T,
    )
    cond, coarse = pl.pallas_call(
        write_out,
        out_shape=(
            jax.ShapeDtypeStruct((SLOTS, ROW), F32),
            jax.ShapeDtypeStruct((4 * OWN, COARSE), F32),
        ),
        in_specs=[vmem] * 2,
        out_specs=(hbm, hbm),
        scratch_shapes=[dma((4,))],
        compiler_params=pltpu.CompilerParams(vmem_limit_bytes=16 * 2**20),
    )(cond, coarse)
    return cond[None, None], coarse[None]


def solution(mesh):
    part = P("dom", "grp", None, None)
    return jax.shard_map(
        body,
        mesh=mesh,
        in_specs=(part, part, part, part, part, P("dom", "grp")),
        out_specs=(part, P("dom", None, None)),
        check_vma=False,
    )
```

```python
import jax
import jax.numpy as jnp
import numpy as np
from jax import lax
from jax.experimental import pallas as pl
from jax.experimental.pallas import tpu as pltpu
from jax.sharding import PartitionSpec as P

F32 = jnp.float32
BF16 = jnp.bfloat16
MESH = pl.DeviceIdType.MESH
ELEMS = 32
NODES = 10
INNER = 64
OWN = 72
SLOTS = 80
ROW = 1280
COARSE = 384
PIECE = 24

NODE_LIST = [(a, b, 3 - a - b) for a in range(4) for b in range(4 - a)]
ORDERINGS = [(0, 1, 2), (1, 2, 0), (2, 0, 1), (0, 2, 1), (2, 1, 0), (1, 0, 2)]
PERM = [
    [NODE_LIST.index((c[p[0]], c[p[1]], c[p[2]])) for c in NODE_LIST] for p in ORDERINGS
]
INVERSE = [[row.index(m) for m in range(NODES)] for row in PERM]
BARY = np.array(NODE_LIST, np.float32) / np.float32(3.0)


def split(x):
    high = x.astype(BF16)
    return high, (x - high.astype(F32)).astype(BF16)


def dot(a, b):
    return jnp.dot(a, b, preferred_element_type=F32)


def iota(shape, dim):
    return lax.broadcasted_iota(jnp.int32, shape, dim)


def spread(small):
    pick = (iota((128, 4), 0) % 4 == iota((128, 4), 1)).astype(F32).astype(BF16)
    rows = dot(pick, small.astype(F32).astype(BF16))
    rows = jnp.where(iota((128, ELEMS), 0) // 4 == iota((128, ELEMS), 1), rows, 0.0)
    return dot(rows.astype(BF16), jnp.ones((ELEMS, 128), BF16))


def oriented(orient, slabs, table, node):
    if all(table[o][node] == node for o in range(6)):
        return slabs[node]
    out = slabs[table[5][node]]
    for o in range(4, -1, -1):
        out = jnp.where(orient == o, slabs[table[o][node]], out)
    return out


def build_selectors(faces_ref, orient_ref, pick_ref, back_ref, turn_ref):
    faces = spread(faces_ref[...])
    turn_ref[...] = spread(orient_ref[...])
    pick = (faces == iota((128, 128), 1).astype(F32)).astype(F32)
    pick_ref[:, :128] = pick.astype(BF16)
    pick_ref[:, 128:] = pick.astype(BF16)
    back = pick.T.astype(BF16)
    back_ref[:, :128] = back
    back_ref[:, 128:] = back


def repeat_fields(value, node, out_ref):
    rows = value.shape[0]
    group = iota(value.shape, 1) // 32
    moved = [value] + [pltpu.roll(value, 32 * s, 1) for s in (1, 2, 3)]
    for field in range(4):
        out = moved[(3 - field) % 4]
        for g in (2, 1, 0):
            out = jnp.where(group == g, moved[(g - field) % 4], out)
        out_ref[pl.ds(node * 4 + field, rows, stride=40), :] = out


def gather_values(local_ref, pick_ref, turn_ref, pieces_ref, values_ref):
    high, low = split(local_ref[...])
    nothing = jnp.zeros((128 - SLOTS, ROW), BF16)
    pieces_ref[0:80, :] = high
    pieces_ref[80:128, :] = nothing
    pieces_ref[128:208, :] = low
    pieces_ref[208:256, :] = nothing
    pick = pick_ref[...]
    slabs = []
    for pair in range(NODES // 2):
        both = dot(pick, pieces_ref[:, pair * 256 : (pair + 1) * 256])
        slabs += [both[:, :128], both[:, 128:]]
    turn = turn_ref[...]
    for node in range(NODES):
        repeat_fields(oriented(turn, slabs, PERM, node), node, values_ref)


def element_product(e, matrix_ref, values):
    lane = iota((40, 128), 1)
    group = lane // 32
    high, low = split(values[:128])
    main = jnp.concatenate([high, low], axis=1)
    main = jnp.concatenate([main, main], axis=0)
    last = values[128:160]
    group32 = iota((32, 128), 1) // 32
    rest = jnp.concatenate([jnp.where(group32 == b, last, 0.0) for b in range(4)], axis=0)
    high, low = split(rest)
    rest = jnp.concatenate([high, low], axis=1)
    rest = jnp.concatenate([rest, rest], axis=0)
    parts = [matrix_ref[e, pl.ds(c, 40, stride=5), :] for c in range(5)]
    rows = [parts[0]]
    for b in range(1, 4):
        mixed = jnp.where(lane >= 32 * b, parts[b], parts[b + 1])
        rows.append(pltpu.roll(mixed, 128 - 32 * b, 1))
    high, low = split(jnp.concatenate(rows, axis=0))
    first = dot(jnp.concatenate([high, low], axis=1), main)
    tail = jnp.where(
        group == 0, parts[1], jnp.where(group == 1, parts[2], jnp.where(group == 2, parts[3], parts[4]))
    )
    high, low = split(tail)
    second = dot(jnp.concatenate([high, low], axis=1), rest)
    first = first[:, :128] + first[:, 128:]
    second = second[:, :128] + second[:, 128:]
    out = jnp.where(
        group == 0,
        first[0:40],
        jnp.where(group == 1, first[40:80], jnp.where(group == 2, first[80:120], first[120:160])),
    )
    return out + second


def scatter_results(result_ref, back_ref, turn_ref, partial_ref):
    turn = turn_ref[...]
    slabs = [result_ref[pl.ds(n, 128, stride=NODES), :] for n in range(NODES)]
    back = back_ref[0:SLOTS, :]
    for pair in range(NODES // 2):
        both = [oriented(turn, slabs, INVERSE, m) for m in (2 * pair, 2 * pair + 1)]
        high, low = split(jnp.concatenate(both, axis=1))
        partial_ref[:, pair * 256 : (pair + 1) * 256] = dot(back, jnp.concatenate([high, low], axis=0))


def add_late(trace_up, low_ref, faces, matrix_ref, pick, back, turn, values_ref, result_ref, partial_ref):
    places = []
    for j in range(8):
        match = faces[...] == OWN + j
        places.append(
            [jnp.max(jnp.where(match, iota((4, ELEMS), dim), 0)) for dim in (1, 0)]
        )
    lower = back[64:SLOTS, :128]
    named = dot(lower, jnp.ones((128, 128), BF16))[8:]
    element = dot(lower, (iota((128, 128), 0) // 4).astype(F32).astype(BF16))[8:]
    turns = turn[...].astype(BF16)
    turn_j = dot(lower, turns)[8:]
    repeat = (iota((32, 8), 0) // 4 == iota((32, 8), 1)).astype(F32).astype(BF16)
    row = dot(repeat, element.astype(BF16)) * 4.0 + (iota((32, 128), 0) % 4).astype(F32)
    chosen = (row == iota((32, 128), 1).astype(F32)).astype(F32).astype(BF16)
    turn_jk = dot(chosen, turns)
    back_jk = dot(chosen, pick[:, :128]).T.astype(BF16)[:SLOTS]
    back_jk = jnp.concatenate([back_jk, back_jk], axis=1)

    trace_up.wait_recv()
    slabs = [
        jnp.where(named > 0.5, low_ref[:, n * 128 : (n + 1) * 128], 0.0) for n in range(NODES)
    ]
    for node in range(NODES):
        repeat_fields(oriented(turn_j, slabs, PERM, node), node, values_ref)
    for j, (e, k) in enumerate(places):
        face = values_ref[j * 40 : (j + 1) * 40, :]
        whole = jnp.concatenate([face * (k == i).astype(F32) for i in range(4)], axis=0)
        result_ref[j * 40 : (j + 1) * 40, :] = element_product(e, matrix_ref, whole)
    slabs = [result_ref[pl.ds(n, 32, stride=NODES), :] for n in range(NODES)]
    for pair in range(NODES // 2):
        both = [oriented(turn_jk, slabs, INVERSE, m) for m in (2 * pair, 2 * pair + 1)]
        high, low = split(jnp.concatenate(both, axis=1))
        part = slice(pair * 256, (pair + 1) * 256)
        partial_ref[:, part] += dot(back_jk, jnp.concatenate([high, low], axis=0))


def project(rows):
    out = []
    for v in range(3):
        terms = [float(BARY[n, v]) * rows(n) for n in range(NODES) if BARY[n, v] != 0]
        total = terms[0]
        for term in terms[1:]:
            total = total + term
        out.append(total)
    return out


def kernel(
    n_dom,
    trace_hbm,
    rhs_hbm,
    matrix_hbm,
    faces_hbm,
    orient_hbm,
    cond_ref,
    coarse_ref,
    local,
    low_trace,
    rhs,
    matrix,
    faces,
    orient,
    pick,
    back,
    turn,
    pieces,
    values,
    result,
    late_values,
    late_result,
    shared,
    arrived,
    low_out,
    low_in,
    in_sem,
    matrix_sem,
    dom_send,
    dom_recv,
    low_send,
    low_recv,
    grp_send,
    grp_recv,
    hello,
):
    d = lax.axis_index("dom")
    g = lax.axis_index("grp")
    has_below = d > 0
    has_above = d < n_dom - 1

    loads = [
        pltpu.make_async_copy(trace_hbm, local.at[pl.ds(0, OWN)], in_sem.at[0]),
        pltpu.make_async_copy(faces_hbm, faces, in_sem.at[1]),
        pltpu.make_async_copy(orient_hbm, orient, in_sem.at[2]),
        pltpu.make_async_copy(rhs_hbm, rhs, in_sem.at[3]),
    ]
    for load in loads[:3]:
        load.start()

    barrier = pltpu.get_barrier_semaphore()

    def greet(dom, grp):
        pl.semaphore_signal(barrier, inc=1, device_id=(dom, grp), device_id_type=MESH)

    @pl.when(has_below)
    def _():
        for i in range(4):
            greet(d - 1, lax.rem(g + i, 4))

    @pl.when(jnp.logical_not(has_below))
    def _():
        for i in range(1, 4):
            greet(d, lax.rem(g + i, 4))

    matrix_loads = [
        pltpu.make_async_copy(matrix_hbm.at[e // 8, :, e % 8, :], matrix.at[e], matrix_sem.at[e])
        for e in range(ELEMS)
    ]
    for load in matrix_loads:
        load.start()
    loads[3].start()

    @pl.when(has_above)
    def _():
        pl.semaphore_wait(barrier, 4 + 3 * (d == 0).astype(jnp.int32))

    def remote(src, dst, send, recv, dom, grp):
        return pltpu.make_async_remote_copy(
            src_ref=src,
            dst_ref=dst,
            send_sem=send,
            recv_sem=recv,
            device_id=(dom, grp),
            device_id_type=MESH,
        )

    trace_up = remote(
        trace_hbm.at[pl.ds(INNER, 8)], low_trace, dom_send.at[0], dom_recv.at[0], d + 1, g
    )
    part_up = remote(shared.at[0], arrived.at[0], dom_send.at[1], dom_recv.at[1], d + 1, g)
    part_down = remote(shared.at[1], arrived.at[1], dom_send.at[2], dom_recv.at[2], d - 1, g)
    low_down = [
        remote(low_out, low_in.at[i], low_send.at[i], low_recv.at[i], d - 1, lax.rem(g + i, 4))
        for i in range(4)
    ]

    @pl.when(has_above)
    def _():
        trace_up.start()
        for i in range(1, 4):
            pl.semaphore_signal(
                hello, inc=1, device_id=(d + 1, lax.rem(g + i, 4)), device_id_type=MESH
            )

    loads[1].wait()
    loads[2].wait()
    build_selectors(faces, orient, pick, back, turn)
    loads[0].wait()

    def all_elements():
        gather_values(local, pick, turn, pieces, values)

        def block(i, carry):
            for q in range(8):
                pltpu.make_async_copy(
                    matrix_hbm.at[0, :, 0, :], matrix.at[i * 8 + q], matrix_sem.at[i * 8 + q]
                ).wait()
            for q in range(8):
                e = i * 8 + q
                result[pl.ds(e * 40, 40), :] = element_product(
                    e, matrix, values[pl.ds(e * 160, 160), :]
                )
            return carry

        lax.fori_loop(0, ELEMS // 8, block, 0)
        scatter_results(result, back, turn, cond_ref)

    local[OWN:SLOTS, :] = jnp.zeros((8, ROW), F32)
    all_elements()

    @pl.when(has_below)
    def _():
        add_late(
            trace_up,
            low_trace,
            faces,
            matrix,
            pick,
            back,
            turn,
            late_values,
            late_result,
            cond_ref,
        )

    shared[0] = cond_ref[INNER:OWN, :]
    shared[1] = cond_ref[OWN:SLOTS, :]

    @pl.when(has_above)
    def _():
        part_up.start()

    @pl.when(has_below)
    def _():
        part_down.start()

    low = project(lambda n: cond_ref[OWN:SLOTS, n * 128 : (n + 1) * 128])
    for v in range(3):
        low_out[:, v * 128 : (v + 1) * 128] = low[v]

    @pl.when(has_below)
    def _():
        pl.semaphore_wait(hello, 3)
        for copy in low_down:
            copy.start()

    loads[3].wait()
    mine = pl.multiple_of(g * OWN, 8)
    own = project(
        lambda n: rhs[:, n * 128 : (n + 1) * 128] - cond_ref[0:OWN, n * 128 : (n + 1) * 128]
    )
    named = dot(back[0:SLOTS, :128], jnp.ones((128, 128), BF16))[:OWN]
    keep = jnp.logical_or(iota((OWN, 128), 0) < INNER, named > 0.5)
    for v in range(3):
        coarse_ref[pl.ds(mine, OWN), v * 128 : (v + 1) * 128] = jnp.where(keep, own[v], 0.0)

    def message(owner, i, n):
        rows = coarse_ref.at[pl.ds(pl.multiple_of(owner * OWN + PIECE * n, 8), PIECE)]
        number = 3 * (i - 1) + n
        to = lax.rem(g + i, 4)
        return remote(rows, rows, grp_send.at[number], grp_recv.at[number], d, to)

    sends = [message(g, i, n) for n in range(OWN // PIECE) for i in (2, 1, 3)]
    for copy in sends:
        copy.start()

    @pl.when(has_above)
    def _():
        part_down.wait_recv()
        cond_ref[INNER:OWN, :] = shared[0] + arrived[1]

    @pl.when(has_below)
    def _():
        part_up.wait_recv()
        cond_ref[OWN:SLOTS, :] = shared[1] + arrived[0]

    for copy in sends:
        copy.wait_send()
    for i in range(1, 4):
        for n in range(OWN // PIECE):
            message(lax.rem(g + 4 - i, 4), i, n).wait_recv()

    @pl.when(has_above)
    def _():
        for i in range(4):
            low_down[i].wait_recv()
            owner = lax.rem(g + 4 - i, 4)
            rows = pl.ds(pl.multiple_of(owner * OWN + INNER, 8), 8)
            coarse_ref[rows, :] = coarse_ref[rows, :] - low_in[i]

    @pl.when(has_above)
    def _():
        trace_up.wait_send()
        part_up.wait_send()

    @pl.when(has_below)
    def _():
        part_down.wait_send()
        for copy in low_down:
            copy.wait_send()


def write_out(cond, coarse, cond_out, coarse_out, sem):
    copies = []
    for half in range(2):
        rows = pl.ds(half * 40, 40)
        copies.append(pltpu.make_async_copy(cond.at[rows], cond_out.at[rows], sem.at[half]))
        rows = pl.ds(half * 144, 144)
        copies.append(pltpu.make_async_copy(coarse.at[rows], coarse_out.at[rows], sem.at[2 + half]))
    for copy in copies:
        copy.start()
    for copy in copies:
        copy.wait()


def body(trace, rhs, stiffness, elem_faces, orient, counts):
    n_dom = lax.axis_size("dom")
    matrix = stiffness.reshape(4, 8, 200, 128).transpose(0, 2, 1, 3)
    hbm = pl.BlockSpec(memory_space=pl.ANY)
    vmem = pl.BlockSpec(memory_space=pltpu.VMEM)
    dma = pltpu.SemaphoreType.DMA
    cond, coarse = pl.pallas_call(
        lambda *refs: kernel(n_dom, *refs),
        out_shape=(
            pltpu.VMEM((SLOTS, ROW), F32),
            pltpu.VMEM((4 * OWN, COARSE), F32),
        ),
        in_specs=[hbm] * 5,
        out_specs=(vmem, vmem),
        scratch_shapes=[
            pltpu.VMEM((SLOTS, ROW), F32),
            pltpu.VMEM((8, ROW), F32),
            pltpu.VMEM((OWN, ROW), F32),
            pltpu.VMEM((ELEMS, 200, 128), F32),
            pltpu.VMEM((4, ELEMS), jnp.int32),
            pltpu.VMEM((4, ELEMS), jnp.int32),
            pltpu.VMEM((128, 256), BF16),
            pltpu.VMEM((128, 256), BF16),
            pltpu.VMEM((128, 128), F32),
            pltpu.VMEM((256, ROW), BF16),
            pltpu.VMEM((ELEMS * 160, 128), F32),
            pltpu.VMEM((ELEMS * 40, 128), F32),
            pltpu.VMEM((8 * 40, 128), F32),
            pltpu.VMEM((8 * 40, 128), F32),
            pltpu.VMEM((2, 8, ROW), F32),
            pltpu.VMEM((2, 8, ROW), F32),
            pltpu.VMEM((8, COARSE), F32),
            pltpu.VMEM((4, 8, COARSE), F32),
            dma((4,)),
            dma((ELEMS,)),
            dma((3,)),
            dma((3,)),
            dma((4,)),
            dma((4,)),
            dma((9,)),
            dma((9,)),
            pltpu.SemaphoreType.REGULAR,
        ],
        compiler_params=pltpu.CompilerParams(
            collective_id=0, has_side_effects=True, vmem_limit_bytes=62_488_000
        ),
    )(
        trace[0, 0],
        rhs[0, 0],
        matrix,
        elem_faces[0, 0].T,
        orient[0, 0].T,
    )
    cond, coarse = pl.pallas_call(
        write_out,
        out_shape=(
            jax.ShapeDtypeStruct((SLOTS, ROW), F32),
            jax.ShapeDtypeStruct((4 * OWN, COARSE), F32),
        ),
        in_specs=[vmem] * 2,
        out_specs=(hbm, hbm),
        scratch_shapes=[dma((4,))],
        compiler_params=pltpu.CompilerParams(vmem_limit_bytes=16 * 2**20),
    )(cond, coarse)
    return cond[None, None], coarse[None]


def solution(mesh):
    part = P("dom", "grp", None, None)
    return jax.shard_map(
        body,
        mesh=mesh,
        in_specs=(part, part, part, part, part, P("dom", "grp")),
        out_specs=(part, P("dom", None, None)),
        check_vma=False,
    )
```

```python
import jax
import jax.numpy as jnp
import numpy as np
from jax import lax
from jax.experimental import pallas as pl
from jax.experimental.pallas import tpu as pltpu
from jax.sharding import PartitionSpec as P

F32 = jnp.float32
BF16 = jnp.bfloat16
MESH = pl.DeviceIdType.MESH
ELEMS = 32
NODES = 10
INNER = 64
OWN = 72
SLOTS = 80
ROW = 1280
COARSE = 384
ROW_LENGTH = 24
PIECE = 24

NODE_LIST = [(a, b, 3 - a - b) for a in range(4) for b in range(4 - a)]
ORDERINGS = [(0, 1, 2), (1, 2, 0), (2, 0, 1), (0, 2, 1), (2, 1, 0), (1, 0, 2)]
PERM = [
    [NODE_LIST.index((c[p[0]], c[p[1]], c[p[2]])) for c in NODE_LIST] for p in ORDERINGS
]
INVERSE = [[row.index(m) for m in range(NODES)] for row in PERM]
BARY = np.array(NODE_LIST, np.float32) / np.float32(3.0)


def split(x):
    high = x.astype(BF16)
    return high, (x - high.astype(F32)).astype(BF16)


def dot(a, b):
    return jnp.dot(a, b, preferred_element_type=F32)


def iota(shape, dim):
    return lax.broadcasted_iota(jnp.int32, shape, dim)


def spread(small):
    pick = (iota((128, 4), 0) % 4 == iota((128, 4), 1)).astype(F32).astype(BF16)
    rows = dot(pick, small.astype(F32).astype(BF16))
    rows = jnp.where(iota((128, ELEMS), 0) // 4 == iota((128, ELEMS), 1), rows, 0.0)
    return dot(rows.astype(BF16), jnp.ones((ELEMS, 128), BF16))


def oriented(orient, slabs, table, node):
    if all(table[o][node] == node for o in range(6)):
        return slabs[node]
    out = slabs[table[5][node]]
    for o in range(4, -1, -1):
        out = jnp.where(orient == o, slabs[table[o][node]], out)
    return out


def build_selectors(faces_ref, orient_ref, pick_ref, back_ref, turn_ref):
    faces = spread(faces_ref[...])
    turn_ref[...] = spread(orient_ref[...])
    pick = (faces == iota((128, 128), 1).astype(F32)).astype(F32)
    pick_ref[:, :128] = pick.astype(BF16)
    pick_ref[:, 128:] = pick.astype(BF16)
    back = pick.T.astype(BF16)
    back_ref[:, :128] = back
    back_ref[:, 128:] = back


def repeat_fields(value, node, out_ref):
    rows = value.shape[0]
    group = iota(value.shape, 1) // 32
    moved = [value] + [pltpu.roll(value, 32 * s, 1) for s in (1, 2, 3)]
    for field in range(4):
        out = moved[(3 - field) % 4]
        for g in (2, 1, 0):
            out = jnp.where(group == g, moved[(g - field) % 4], out)
        out_ref[pl.ds(node * 4 + field, rows, stride=40), :] = out


def gather_values(local_ref, pick_ref, turn_ref, pieces_ref, values_ref):
    high, low = split(local_ref[...])
    nothing = jnp.zeros((128 - SLOTS, ROW), BF16)
    pieces_ref[0:80, :] = high
    pieces_ref[80:128, :] = nothing
    pieces_ref[128:208, :] = low
    pieces_ref[208:256, :] = nothing
    pick = pick_ref[...]
    slabs = []
    for pair in range(NODES // 2):
        both = dot(pick, pieces_ref[:, pair * 256 : (pair + 1) * 256])
        slabs += [both[:, :128], both[:, 128:]]
    turn = turn_ref[...]
    for node in range(NODES):
        repeat_fields(oriented(turn, slabs, PERM, node), node, values_ref)


def element_product(e, matrix_ref, values):
    lane = iota((40, 128), 1)
    group = lane // 32
    high, low = split(values[:128])
    main = jnp.concatenate([high, low], axis=1)
    main = jnp.concatenate([main, main], axis=0)
    last = values[128:160]
    group32 = iota((32, 128), 1) // 32
    rest = jnp.concatenate([jnp.where(group32 == b, last, 0.0) for b in range(4)], axis=0)
    high, low = split(rest)
    rest = jnp.concatenate([high, low], axis=1)
    rest = jnp.concatenate([rest, rest], axis=0)
    parts = [matrix_ref[e, pl.ds(c, 40, stride=5), :] for c in range(5)]
    rows = [parts[0]]
    for b in range(1, 4):
        mixed = jnp.where(lane >= 32 * b, parts[b], parts[b + 1])
        rows.append(pltpu.roll(mixed, 128 - 32 * b, 1))
    high, low = split(jnp.concatenate(rows, axis=0))
    first = dot(jnp.concatenate([high, low], axis=1), main)
    tail = jnp.where(
        group == 0, parts[1], jnp.where(group == 1, parts[2], jnp.where(group == 2, parts[3], parts[4]))
    )
    high, low = split(tail)
    second = dot(jnp.concatenate([high, low], axis=1), rest)
    first = first[:, :128] + first[:, 128:]
    second = second[:, :128] + second[:, 128:]
    out = jnp.where(
        group == 0,
        first[0:40],
        jnp.where(group == 1, first[40:80], jnp.where(group == 2, first[80:120], first[120:160])),
    )
    return out + second


def scatter_results(result_ref, back_ref, turn_ref, partial_ref):
    turn = turn_ref[...]
    slabs = [result_ref[pl.ds(n, 128, stride=NODES), :] for n in range(NODES)]
    back = back_ref[0:SLOTS, :]
    for pair in range(NODES // 2):
        both = [oriented(turn, slabs, INVERSE, m) for m in (2 * pair, 2 * pair + 1)]
        high, low = split(jnp.concatenate(both, axis=1))
        partial_ref[:, pair * 256 : (pair + 1) * 256] = dot(back, jnp.concatenate([high, low], axis=0))


def prepare_late(faces, pick, back, turn):
    places = []
    for j in range(8):
        match = faces[...] == OWN + j
        places.append([jnp.max(jnp.where(match, iota((4, ELEMS), dim), 0)) for dim in (1, 0)])
    lower = back[64:SLOTS, :128]
    named = dot(lower, jnp.ones((128, 128), BF16))[8:]
    element = dot(lower, (iota((128, 128), 0) // 4).astype(F32).astype(BF16))[8:]
    turns = turn[...].astype(BF16)
    turn_j = dot(lower, turns)[8:]
    repeat = (iota((128, 8), 0) % 32 // 4 == iota((128, 8), 1)).astype(F32).astype(BF16)
    row = dot(repeat, element.astype(BF16)) * 4.0 + (iota((128, 128), 0) % 4).astype(F32)
    chosen = (row == iota((128, 128), 1).astype(F32)).astype(F32).astype(BF16)
    turn_jk = dot(chosen, turns)[:32]
    back_jk = dot(chosen, pick[:, :128]).T.astype(BF16)
    slots = dot(iota((8, 128), 1).astype(F32).astype(BF16), back_jk)
    slots = jnp.where(iota((8, 128), 1) < 64, slots, -1.0)
    return places, named, turn_j, turn_jk, back_jk[:SLOTS, :64], slots


def late_products(places, named, turn_j, turn_jk, low_ref, matrix_ref, values_ref, result_ref, rows_ref):
    slabs = [
        jnp.where(named > 0.5, low_ref[:, n * 128 : (n + 1) * 128], 0.0) for n in range(NODES)
    ]
    for node in range(NODES):
        repeat_fields(oriented(turn_j, slabs, PERM, node), node, values_ref)
    for j, (e, k) in enumerate(places):
        face = values_ref[j * 40 : (j + 1) * 40, :]
        whole = jnp.concatenate([face * (k == i).astype(F32) for i in range(4)], axis=0)
        result_ref[j * 40 : (j + 1) * 40, :] = element_product(e, matrix_ref, whole)
    slabs = [result_ref[pl.ds(n, 32, stride=NODES), :] for n in range(NODES)]
    for node in range(NODES):
        rows_ref[:, node * 128 : (node + 1) * 128] = oriented(turn_jk, slabs, INVERSE, node)


def add_rows(back_jk, rows_ref, partial_ref):
    for pair in range(NODES // 2):
        part = slice(pair * 256, (pair + 1) * 256)
        high, low = split(rows_ref[:, part])
        partial_ref[:, part] += dot(back_jk, jnp.concatenate([high, low], axis=0))


def project(rows):
    out = []
    for v in range(3):
        terms = [float(BARY[n, v]) * rows(n) for n in range(NODES) if BARY[n, v] != 0]
        total = terms[0]
        for term in terms[1:]:
            total = total + term
        out.append(total)
    return out


def kernel(
    n_dom,
    trace_hbm,
    rhs_hbm,
    matrix_hbm,
    faces_hbm,
    orient_hbm,
    cond_ref,
    coarse_ref,
    local,
    low_trace,
    rhs,
    matrix,
    faces,
    orient,
    pick,
    back,
    turn,
    pieces,
    values,
    result,
    late_values,
    late_result,
    late_rows,
    slots,
    extra,
    shared,
    arrived,
    low_out,
    low_in,
    in_sem,
    matrix_sem,
    dom_send,
    dom_recv,
    low_send,
    low_recv,
    grp_send,
    grp_recv,
    hello,
    hello_back,
    slot_send,
    slot_recv,
    extra_send,
    extra_recv,
):
    d = lax.axis_index("dom")
    g = lax.axis_index("grp")
    has_below = d > 0
    has_above = d < n_dom - 1

    loads = [
        pltpu.make_async_copy(trace_hbm, local.at[pl.ds(0, OWN)], in_sem.at[0]),
        pltpu.make_async_copy(faces_hbm, faces, in_sem.at[1]),
        pltpu.make_async_copy(orient_hbm, orient, in_sem.at[2]),
        pltpu.make_async_copy(rhs_hbm, rhs, in_sem.at[3]),
    ]
    for load in loads[:3]:
        load.start()

    barrier = pltpu.get_barrier_semaphore()

    def greet(dom, grp):
        pl.semaphore_signal(barrier, inc=1, device_id=(dom, grp), device_id_type=MESH)

    @pl.when(has_below)
    def _():
        for i in range(4):
            greet(d - 1, lax.rem(g + i, 4))

    @pl.when(jnp.logical_not(has_below))
    def _():
        for i in range(1, 4):
            greet(d, lax.rem(g + i, 4))

    matrix_loads = [
        pltpu.make_async_copy(matrix_hbm.at[e // 8, :, e % 8, :], matrix.at[e], matrix_sem.at[e])
        for e in range(ELEMS)
    ]
    @pl.when(has_above)
    def _():
        pl.semaphore_wait(barrier, 4 + 3 * (d == 0).astype(jnp.int32))

    def remote(src, dst, send, recv, dom, grp):
        return pltpu.make_async_remote_copy(
            src_ref=src,
            dst_ref=dst,
            send_sem=send,
            recv_sem=recv,
            device_id=(dom, grp),
            device_id_type=MESH,
        )

    trace_up = remote(
        trace_hbm.at[pl.ds(INNER, 8)], low_trace, dom_send.at[0], dom_recv.at[0], d + 1, g
    )
    part_up = remote(shared.at[0], arrived.at[0], dom_send.at[1], dom_recv.at[1], d + 1, g)
    part_down = remote(shared.at[1], arrived.at[1], dom_send.at[2], dom_recv.at[2], d - 1, g)
    low_down = [
        remote(low_out, low_in.at[i], low_send.at[i], low_recv.at[i], d - 1, lax.rem(g + i, 4))
        for i in range(4)
    ]

    @pl.when(has_above)
    def _():
        trace_up.start()
        for i in range(1, 4):
            pl.semaphore_signal(
                hello, inc=1, device_id=(d + 1, lax.rem(g + i, 4)), device_id_type=MESH
            )

    for load in matrix_loads:
        load.start()
    loads[3].start()
    loads[1].wait()
    loads[2].wait()
    build_selectors(faces, orient, pick, back, turn)
    loads[0].wait()

    def all_elements():
        gather_values(local, pick, turn, pieces, values)

        def block(i, carry):
            for q in range(8):
                pltpu.make_async_copy(
                    matrix_hbm.at[0, :, 0, :], matrix.at[i * 8 + q], matrix_sem.at[i * 8 + q]
                ).wait()
            for q in range(8):
                e = i * 8 + q
                result[pl.ds(e * 40, 40), :] = element_product(
                    e, matrix, values[pl.ds(e * 160, 160), :]
                )
            return carry

        lax.fori_loop(0, ELEMS // 8, block, 0)
        scatter_results(result, back, turn, cond_ref)

    local[OWN:SLOTS, :] = jnp.zeros((8, ROW), F32)
    all_elements()
    loads[3].wait()
    mine = pl.multiple_of(g * OWN, 8)

    def own_coarse():
        own = project(
            lambda n: rhs[:, n * 128 : (n + 1) * 128] - cond_ref[0:OWN, n * 128 : (n + 1) * 128]
        )
        named = dot(back[0:SLOTS, :128], jnp.ones((128, 128), BF16))[:OWN]
        keep = jnp.logical_or(iota((OWN, 128), 0) < INNER, named > 0.5)
        for v in range(3):
            coarse_ref[pl.ds(mine, OWN), v * 128 : (v + 1) * 128] = jnp.where(keep, own[v], 0.0)

    def message(owner, i, n):
        rows = coarse_ref.at[pl.ds(pl.multiple_of(owner * OWN + PIECE * n, 8), PIECE)]
        number = 3 * (i - 1) + n
        to = lax.rem(g + i, 4)
        return remote(rows, rows, grp_send.at[number], grp_recv.at[number], d, to)

    def to_peer(array, send, recv, i):
        return remote(
            array.at[0], array.at[i], send.at[i - 1], recv.at[i - 1], d, lax.rem(g + i, 4)
        )

    sends = [message(g, i, n) for n in range(OWN // PIECE) for i in (2, 1, 3)]
    slot_sends = [to_peer(slots, slot_send, slot_recv, i) for i in (2, 1, 3)]
    extra_sends = [to_peer(extra, extra_send, extra_recv, i) for i in (2, 1, 3)]

    place = lax.rem(d, ROW_LENGTH)
    ahead = jnp.logical_and(place == 0, has_below)
    after_ahead = jnp.logical_and(place == 1, d > 1)

    @pl.when(has_below)
    def _():
        places, named, turn_j, turn_jk, back_jk, slot_row = prepare_late(faces, pick, back, turn)

        @pl.when(ahead)
        def _():
            own_coarse()
            slots[0] = slot_row
            pl.semaphore_wait(hello_back, 1)
            for copy in sends:
                copy.start()
            for copy in slot_sends:
                copy.start()

        trace_up.wait_recv()

        @pl.when(after_ahead)
        def _():
            pl.semaphore_wait(hello, 3)
            pl.semaphore_signal(hello_back, inc=1, device_id=(d - 1, g), device_id_type=MESH)

        late_products(
            places, named, turn_j, turn_jk, low_trace, matrix, late_values, late_result, late_rows
        )

        @pl.when(ahead)
        def _():
            more = project(lambda n: late_rows[:, n * 128 : (n + 1) * 128])
            for v in range(3):
                extra[0, :, v * 128 : (v + 1) * 128] = more[v]
            for copy in extra_sends:
                copy.start()

        add_rows(back_jk, late_rows, cond_ref)

    shared[0] = cond_ref[INNER:OWN, :]
    shared[1] = cond_ref[OWN:SLOTS, :]

    @pl.when(has_above)
    def _():
        part_up.start()

    @pl.when(has_below)
    def _():
        part_down.start()

    low = project(lambda n: cond_ref[OWN:SLOTS, n * 128 : (n + 1) * 128])
    for v in range(3):
        low_out[:, v * 128 : (v + 1) * 128] = low[v]

    @pl.when(has_below)
    def _():
        @pl.when(jnp.logical_not(after_ahead))
        def _():
            pl.semaphore_wait(hello, 3)

        for copy in low_down:
            copy.start()

    @pl.when(jnp.logical_not(ahead))
    def _():
        own_coarse()
        for copy in sends:
            copy.start()

    @pl.when(has_above)
    def _():
        part_down.wait_recv()
        cond_ref[INNER:OWN, :] = shared[0] + arrived[1]

    @pl.when(has_below)
    def _():
        part_up.wait_recv()
        cond_ref[OWN:SLOTS, :] = shared[1] + arrived[0]

    for copy in sends:
        copy.wait_send()
    for i in range(1, 4):
        for n in range(OWN // PIECE):
            message(lax.rem(g + 4 - i, 4), i, n).wait_recv()

    @pl.when(ahead)
    def _():
        for copy in slot_sends + extra_sends:
            copy.wait()
        for i in range(4):
            rows = pl.ds(pl.multiple_of(lax.rem(g + 4 - i, 4) * OWN, 8), OWN)
            target = iota((OWN, 128), 0).astype(F32) == slots[i, 0:1, :]
            high, low = split(extra[i])
            more = dot(
                target.astype(F32).astype(BF16)[:, :64], jnp.concatenate([high, low], axis=0)
            )
            coarse_ref[rows, :] = coarse_ref[rows, :] - more

    @pl.when(has_above)
    def _():
        for i in range(4):
            low_down[i].wait_recv()
            owner = lax.rem(g + 4 - i, 4)
            rows = pl.ds(pl.multiple_of(owner * OWN + INNER, 8), 8)
            coarse_ref[rows, :] = coarse_ref[rows, :] - low_in[i]

    @pl.when(has_above)
    def _():
        trace_up.wait_send()
        part_up.wait_send()

    @pl.when(has_below)
    def _():
        part_down.wait_send()
        for copy in low_down:
            copy.wait_send()


def write_out(cond, coarse, cond_out, coarse_out, sem):
    copies = []
    for half in range(2):
        rows = pl.ds(half * 40, 40)
        copies.append(pltpu.make_async_copy(cond.at[rows], cond_out.at[rows], sem.at[half]))
        rows = pl.ds(half * 144, 144)
        copies.append(pltpu.make_async_copy(coarse.at[rows], coarse_out.at[rows], sem.at[2 + half]))
    for copy in copies:
        copy.start()
    for copy in copies:
        copy.wait()


def body(trace, rhs, stiffness, elem_faces, orient, counts):
    n_dom = lax.axis_size("dom")
    matrix = stiffness.reshape(4, 8, 200, 128).transpose(0, 2, 1, 3)
    hbm = pl.BlockSpec(memory_space=pl.ANY)
    vmem = pl.BlockSpec(memory_space=pltpu.VMEM)
    dma = pltpu.SemaphoreType.DMA
    cond, coarse = pl.pallas_call(
        lambda *refs: kernel(n_dom, *refs),
        out_shape=(
            pltpu.VMEM((SLOTS, ROW), F32),
            pltpu.VMEM((4 * OWN, COARSE), F32),
        ),
        in_specs=[hbm] * 5,
        out_specs=(vmem, vmem),
        scratch_shapes=[
            pltpu.VMEM((SLOTS, ROW), F32),
            pltpu.VMEM((8, ROW), F32),
            pltpu.VMEM((OWN, ROW), F32),
            pltpu.VMEM((ELEMS, 200, 128), F32),
            pltpu.VMEM((4, ELEMS), jnp.int32),
            pltpu.VMEM((4, ELEMS), jnp.int32),
            pltpu.VMEM((128, 256), BF16),
            pltpu.VMEM((128, 256), BF16),
            pltpu.VMEM((128, 128), F32),
            pltpu.VMEM((256, ROW), BF16),
            pltpu.VMEM((ELEMS * 160, 128), F32),
            pltpu.VMEM((ELEMS * 40, 128), F32),
            pltpu.VMEM((8 * 40, 128), F32),
            pltpu.VMEM((8 * 40, 128), F32),
            pltpu.VMEM((32, ROW), F32),
            pltpu.VMEM((4, 8, 128), F32),
            pltpu.VMEM((4, 32, COARSE), F32),
            pltpu.VMEM((2, 8, ROW), F32),
            pltpu.VMEM((2, 8, ROW), F32),
            pltpu.VMEM((8, COARSE), F32),
            pltpu.VMEM((4, 8, COARSE), F32),
            dma((4,)),
            dma((ELEMS,)),
            dma((3,)),
            dma((3,)),
            dma((4,)),
            dma((4,)),
            dma((9,)),
            dma((9,)),
            pltpu.SemaphoreType.REGULAR,
            pltpu.SemaphoreType.REGULAR,
            dma((3,)),
            dma((3,)),
            dma((3,)),
            dma((3,)),
        ],
        compiler_params=pltpu.CompilerParams(
            collective_id=0, has_side_effects=True, vmem_limit_bytes=62_488_000
        ),
    )(
        trace[0, 0],
        rhs[0, 0],
        matrix,
        elem_faces[0, 0].T,
        orient[0, 0].T,
    )
    cond, coarse = pl.pallas_call(
        write_out,
        out_shape=(
            jax.ShapeDtypeStruct((SLOTS, ROW), F32),
            jax.ShapeDtypeStruct((4 * OWN, COARSE), F32),
        ),
        in_specs=[vmem] * 2,
        out_specs=(hbm, hbm),
        scratch_shapes=[dma((4,))],
        compiler_params=pltpu.CompilerParams(vmem_limit_bytes=16 * 2**20),
    )(cond, coarse)
    return cond[None, None], coarse[None]


def solution(mesh):
    part = P("dom", "grp", None, None)
    return jax.shard_map(
        body,
        mesh=mesh,
        in_specs=(part, part, part, part, part, P("dom", "grp")),
        out_specs=(part, P("dom", None, None)),
        check_vma=False,
    )
```

```python
import jax
import jax.numpy as jnp
import numpy as np
from jax import lax
from jax.experimental import pallas as pl
from jax.experimental.pallas import tpu as pltpu
from jax.sharding import PartitionSpec as P

F32 = jnp.float32
BF16 = jnp.bfloat16
MESH = pl.DeviceIdType.MESH
ELEMS = 32
NODES = 10
INNER = 64
OWN = 72
SLOTS = 80
ROW = 1280
COARSE = 384
ROW_LENGTH = 24
PIECE = 24

NODE_LIST = [(a, b, 3 - a - b) for a in range(4) for b in range(4 - a)]
ORDERINGS = [(0, 1, 2), (1, 2, 0), (2, 0, 1), (0, 2, 1), (2, 1, 0), (1, 0, 2)]
PERM = [
    [NODE_LIST.index((c[p[0]], c[p[1]], c[p[2]])) for c in NODE_LIST] for p in ORDERINGS
]
INVERSE = [[row.index(m) for m in range(NODES)] for row in PERM]
BARY = np.array(NODE_LIST, np.float32) / np.float32(3.0)


def split(x):
    high = x.astype(BF16)
    return high, (x - high.astype(F32)).astype(BF16)


def dot(a, b):
    return jnp.dot(a, b, preferred_element_type=F32)


def iota(shape, dim):
    return lax.broadcasted_iota(jnp.int32, shape, dim)


def spread(small):
    pick = (iota((128, 4), 0) % 4 == iota((128, 4), 1)).astype(F32).astype(BF16)
    rows = dot(pick, small.astype(F32).astype(BF16))
    rows = jnp.where(iota((128, ELEMS), 0) // 4 == iota((128, ELEMS), 1), rows, 0.0)
    return dot(rows.astype(BF16), jnp.ones((ELEMS, 128), BF16))


def oriented(orient, slabs, table, node):
    if all(table[o][node] == node for o in range(6)):
        return slabs[node]
    out = slabs[table[5][node]]
    for o in range(4, -1, -1):
        out = jnp.where(orient == o, slabs[table[o][node]], out)
    return out


def build_selectors(faces_ref, orient_ref, pick_ref, back_ref, turn_ref):
    faces = spread(faces_ref[...])
    turn_ref[...] = spread(orient_ref[...])
    pick = (faces == iota((128, 128), 1).astype(F32)).astype(F32)
    pick_ref[:, :128] = pick.astype(BF16)
    pick_ref[:, 128:] = pick.astype(BF16)
    back = pick.T.astype(BF16)
    back_ref[:, :128] = back
    back_ref[:, 128:] = back


def repeat_fields(value, node, out_ref):
    rows = value.shape[0]
    group = iota(value.shape, 1) // 32
    moved = [value] + [pltpu.roll(value, 32 * s, 1) for s in (1, 2, 3)]
    for field in range(4):
        out = moved[(3 - field) % 4]
        for g in (2, 1, 0):
            out = jnp.where(group == g, moved[(g - field) % 4], out)
        out_ref[pl.ds(node * 4 + field, rows, stride=40), :] = out


def gather_values(local_ref, pick_ref, turn_ref, pieces_ref, values_ref):
    high, low = split(local_ref[...])
    nothing = jnp.zeros((128 - SLOTS, ROW), BF16)
    pieces_ref[0:80, :] = high
    pieces_ref[80:128, :] = nothing
    pieces_ref[128:208, :] = low
    pieces_ref[208:256, :] = nothing
    pick = pick_ref[...]
    slabs = []
    for pair in range(NODES // 2):
        both = dot(pick, pieces_ref[:, pair * 256 : (pair + 1) * 256])
        slabs += [both[:, :128], both[:, 128:]]
    turn = turn_ref[...]
    for node in range(NODES):
        repeat_fields(oriented(turn, slabs, PERM, node), node, values_ref)


def matrix_pieces(e, matrix_ref):
    lane = iota((40, 128), 1)
    group = lane // 32
    parts = [matrix_ref[e, pl.ds(c, 40, stride=5), :] for c in range(5)]
    rows = [parts[0]]
    for b in range(1, 4):
        mixed = jnp.where(lane >= 32 * b, parts[b], parts[b + 1])
        rows.append(pltpu.roll(mixed, 128 - 32 * b, 1))
    high, low = split(jnp.concatenate(rows, axis=0))
    main = jnp.concatenate([high, low], axis=1)
    tail = jnp.where(
        group == 0, parts[1], jnp.where(group == 1, parts[2], jnp.where(group == 2, parts[3], parts[4]))
    )
    return main, tail


def value_pieces(values):
    high, low = split(values[:128])
    main = jnp.concatenate([high, low], axis=1)
    main = jnp.concatenate([main, main], axis=0)
    last = values[128:160]
    group = iota((32, 128), 1) // 32
    rest = jnp.concatenate([jnp.where(group == b, last, 0.0) for b in range(4)], axis=0)
    high, low = split(rest)
    rest = jnp.concatenate([high, low], axis=1)
    return main, jnp.concatenate([rest, rest], axis=0)


def pieces_product(matrix_main, matrix_tail, values):
    main, rest = value_pieces(values)
    first = dot(matrix_main, main)
    second = dot(matrix_tail, rest)[:40]
    first = first[:, :128] + first[:, 128:]
    second = second[:, :128] + second[:, 128:]
    group = iota((40, 128), 1) // 32
    out = jnp.where(
        group == 0,
        first[0:40],
        jnp.where(group == 1, first[40:80], jnp.where(group == 2, first[80:120], first[120:160])),
    )
    return out + second


def element_product(e, matrix_ref, values):
    main, tail = matrix_pieces(e, matrix_ref)
    high, low = split(tail)
    return pieces_product(main, jnp.concatenate([high, low], axis=1), values)


def scatter_results(result_ref, back_ref, turn_ref, partial_ref):
    turn = turn_ref[...]
    slabs = [result_ref[pl.ds(n, 128, stride=NODES), :] for n in range(NODES)]
    back = back_ref[0:SLOTS, :]
    for pair in range(NODES // 2):
        both = [oriented(turn, slabs, INVERSE, m) for m in (2 * pair, 2 * pair + 1)]
        high, low = split(jnp.concatenate(both, axis=1))
        partial_ref[:, pair * 256 : (pair + 1) * 256] = dot(back, jnp.concatenate([high, low], axis=0))


def prepare_late(faces, pick, back, turn, start):
    places = []
    for j in range(8):
        match = faces[...] == start + j
        places.append([jnp.max(jnp.where(match, iota((4, ELEMS), dim), 0)) for dim in (1, 0)])
    lower = back[64:SLOTS, :128]
    part = slice(start - 64, start - 56)
    named = dot(lower, jnp.ones((128, 128), BF16))[part]
    element = dot(lower, (iota((128, 128), 0) // 4).astype(F32).astype(BF16))[part]
    face = dot(lower, (iota((128, 128), 0) % 4).astype(F32).astype(BF16))[part]
    turns = turn[...].astype(BF16)
    turn_j = dot(lower, turns)[part]
    repeat = (iota((128, 8), 0) % 32 // 4 == iota((128, 8), 1)).astype(F32).astype(BF16)
    row = dot(repeat, element.astype(BF16)) * 4.0 + (iota((128, 128), 0) % 4).astype(F32)
    chosen = (row == iota((128, 128), 1).astype(F32)).astype(F32).astype(BF16)
    turn_jk = dot(chosen, turns)[:32]
    back_jk = dot(chosen, pick[:, :128]).T.astype(BF16)
    slots = dot(iota((8, 128), 1).astype(F32).astype(BF16), back_jk)
    slots = jnp.where(iota((8, 128), 1) < 64, slots, -1.0)
    return places, named, face, turn_j, turn_jk, back_jk[:SLOTS, :64], slots


def owned_products(places, named, face, turn_jk, matrix_ref, values_ref, result_ref, rows_ref, out_ref):
    for j, (e, k) in enumerate(places):
        values = values_ref[pl.ds(e * 160, 160), :]
        result_ref[j * 40 : (j + 1) * 40, :] = element_product(e, matrix_ref, values)
    late_to_slots(turn_jk, result_ref, rows_ref)
    lane = iota((8, 128), 1) % 32
    own = jnp.logical_and(lane // 4 == iota((8, 128), 0), (lane % 4).astype(F32) == face)
    own = jnp.where(jnp.logical_and(own, named > 0.5), 1.0, 0.0)
    own = jnp.concatenate([own, jnp.zeros((8, 128), F32)], axis=0).astype(BF16)[:, :64]
    for pair in range(NODES // 2):
        part = slice(pair * 256, (pair + 1) * 256)
        high, low = split(rows_ref[:, part])
        out_ref[:, part] = dot(own, jnp.concatenate([high, low], axis=0))[:8]


def prepare_matrices(places, matrix_ref, ready_ref):
    for j, (e, k) in enumerate(places):
        main, tail = matrix_pieces(e, matrix_ref)
        high, low = split(jnp.concatenate([tail, jnp.zeros((8, 128), F32)], axis=0))
        ready_ref[j, 0:160, :] = main
        ready_ref[j, 160:208, :] = jnp.concatenate([high, low], axis=1)


def late_products(places, named, turn_j, low_ref, ready_ref, values_ref, result_ref):
    slabs = [
        jnp.where(named > 0.5, low_ref[:, n * 128 : (n + 1) * 128], 0.0) for n in range(NODES)
    ]
    for node in range(NODES):
        repeat_fields(oriented(turn_j, slabs, PERM, node), node, values_ref)
    for j, (e, k) in enumerate(places):
        face = values_ref[j * 40 : (j + 1) * 40, :]
        whole = jnp.concatenate([face * (k == i).astype(F32) for i in range(4)], axis=0)
        result_ref[j * 40 : (j + 1) * 40, :] = pieces_product(
            ready_ref[j, 0:160, :], ready_ref[j, 160:208, :], whole
        )


def late_to_slots(turn_jk, result_ref, rows_ref):
    slabs = [result_ref[pl.ds(n, 32, stride=NODES), :] for n in range(NODES)]
    for node in range(NODES):
        rows_ref[:, node * 128 : (node + 1) * 128] = oriented(turn_jk, slabs, INVERSE, node)


def add_rows(back_jk, rows_ref, partial_ref, start, stop):
    for pair in range(NODES // 2):
        part = slice(pair * 256, (pair + 1) * 256)
        high, low = split(rows_ref[:, part])
        partial_ref[start:stop, part] += dot(
            back_jk[start:stop], jnp.concatenate([high, low], axis=0)
        )


def project_late(turn_jk, result_ref):
    slabs = [result_ref[pl.ds(n, 32, stride=NODES), :] for n in range(NODES)]
    corners = project(lambda n: slabs[n])
    out = []
    for v in range(3):
        row = corners[ORDERINGS[5][v]]
        for o in range(4, -1, -1):
            row = jnp.where(turn_jk == o, corners[ORDERINGS[o][v]], row)
        out.append(row)
    return out


def project(rows):
    out = []
    for v in range(3):
        terms = [float(BARY[n, v]) * rows(n) for n in range(NODES) if BARY[n, v] != 0]
        total = terms[0]
        for term in terms[1:]:
            total = total + term
        out.append(total)
    return out


def kernel(
    n_dom,
    trace_hbm,
    rhs_hbm,
    matrix_hbm,
    faces_hbm,
    orient_hbm,
    cond_ref,
    coarse_ref,
    local,
    low_trace,
    rhs,
    matrix,
    faces,
    orient,
    pick,
    back,
    turn,
    pieces,
    values,
    result,
    late_values,
    late_result,
    late_rows,
    early,
    ready,
    slots,
    extra,
    shared,
    arrived,
    low_out,
    low_in,
    in_sem,
    matrix_sem,
    dom_send,
    dom_recv,
    low_send,
    low_recv,
    grp_send,
    grp_recv,
    hello,
    hello_back,
    slot_send,
    slot_recv,
    extra_send,
    extra_recv,
):
    d = lax.axis_index("dom")
    g = lax.axis_index("grp")
    has_below = d > 0
    has_above = d < n_dom - 1

    loads = [
        pltpu.make_async_copy(trace_hbm, local.at[pl.ds(0, OWN)], in_sem.at[0]),
        pltpu.make_async_copy(faces_hbm, faces, in_sem.at[1]),
        pltpu.make_async_copy(orient_hbm, orient, in_sem.at[2]),
        pltpu.make_async_copy(rhs_hbm, rhs, in_sem.at[3]),
    ]
    for load in loads[:3]:
        load.start()

    barrier = pltpu.get_barrier_semaphore()

    def greet(dom, grp):
        pl.semaphore_signal(barrier, inc=1, device_id=(dom, grp), device_id_type=MESH)

    @pl.when(has_below)
    def _():
        for i in range(4):
            greet(d - 1, lax.rem(g + i, 4))

    @pl.when(jnp.logical_not(has_below))
    def _():
        for i in range(1, 4):
            greet(d, lax.rem(g + i, 4))

    matrix_loads = [
        pltpu.make_async_copy(matrix_hbm.at[e // 8, :, e % 8, :], matrix.at[e], matrix_sem.at[e])
        for e in range(ELEMS)
    ]
    @pl.when(has_above)
    def _():
        pl.semaphore_wait(barrier, 4 + 3 * (d == 0).astype(jnp.int32))

    def remote(src, dst, send, recv, dom, grp):
        return pltpu.make_async_remote_copy(
            src_ref=src,
            dst_ref=dst,
            send_sem=send,
            recv_sem=recv,
            device_id=(dom, grp),
            device_id_type=MESH,
        )

    trace_up = remote(
        trace_hbm.at[pl.ds(INNER, 8)], low_trace, dom_send.at[0], dom_recv.at[0], d + 1, g
    )
    part_up = remote(shared.at[0], arrived.at[0], dom_send.at[1], dom_recv.at[1], d + 1, g)
    part_down = remote(shared.at[1], arrived.at[1], dom_send.at[2], dom_recv.at[2], d - 1, g)
    low_down = [
        remote(low_out, low_in.at[i], low_send.at[i], low_recv.at[i], d - 1, lax.rem(g + i, 4))
        for i in range(4)
    ]

    @pl.when(has_above)
    def _():
        trace_up.start()
        for i in range(1, 4):
            pl.semaphore_signal(
                hello, inc=1, device_id=(d + 1, lax.rem(g + i, 4)), device_id_type=MESH
            )

    for load in matrix_loads + loads[3:]:
        load.start()
    loads[1].wait()
    loads[2].wait()
    build_selectors(faces, orient, pick, back, turn)
    loads[0].wait()

    place = lax.rem(d, ROW_LENGTH)
    ahead = jnp.logical_and(place == 0, has_below)
    after_ahead = jnp.logical_and(place == 1, d > 1)
    tail = jnp.logical_and(place == ROW_LENGTH - 1, has_above)
    not_tail = jnp.logical_not(tail)

    def late_part(ready_late):
        places, named, face, turn_j, turn_jk, back_jk, slot_row = ready_late
        prepare_matrices(places, matrix, ready)
        trace_up.wait_recv()
        late_products(places, named, turn_j, low_trace, ready, late_values, late_result)

    def owned_first():
        for load in matrix_loads:
            load.wait()
        places, named, face, turn_j, turn_jk, back_jk, slot_row = prepare_late(
            faces, pick, back, turn, INNER
        )
        owned_products(
            places, named, face, turn_jk, matrix, values, late_result, late_rows, early
        )
        ready_late = prepare_late(faces, pick, back, turn, OWN)
        late_part(ready_late)
        late_to_slots(ready_late[4], late_result, late_rows)
        back_jk = ready_late[5][INNER:SLOTS]
        for pair in range(NODES // 2):
            part = slice(pair * 256, (pair + 1) * 256)
            high, low = split(late_rows[:, part])
            more = dot(back_jk, jnp.concatenate([high, low], axis=0))[:8]
            shared[0, :, part] = early[:, part] + more
        part_up.start()

    def all_elements():
        gather_values(local, pick, turn, pieces, values)
        pl.when(tail)(owned_first)

        def block(i, carry):
            @pl.when(not_tail)
            def _():
                for q in range(8):
                    pltpu.make_async_copy(
                        matrix_hbm.at[0, :, 0, :], matrix.at[i * 8 + q], matrix_sem.at[i * 8 + q]
                    ).wait()

            for q in range(8):
                e = i * 8 + q
                result[pl.ds(e * 40, 40), :] = element_product(
                    e, matrix, values[pl.ds(e * 160, 160), :]
                )
            return carry

        lax.fori_loop(0, ELEMS // 8, block, 0)
        scatter_results(result, back, turn, cond_ref)

    local[OWN:SLOTS, :] = jnp.zeros((8, ROW), F32)
    all_elements()
    loads[3].wait()
    mine = pl.multiple_of(g * OWN, 8)

    def own_coarse():
        own = project(
            lambda n: rhs[:, n * 128 : (n + 1) * 128] - cond_ref[0:OWN, n * 128 : (n + 1) * 128]
        )
        named = dot(back[0:SLOTS, :128], jnp.ones((128, 128), BF16))[:OWN]
        keep = jnp.logical_or(iota((OWN, 128), 0) < INNER, named > 0.5)
        for v in range(3):
            coarse_ref[pl.ds(mine, OWN), v * 128 : (v + 1) * 128] = jnp.where(keep, own[v], 0.0)

    def message(owner, i, n):
        rows = coarse_ref.at[pl.ds(pl.multiple_of(owner * OWN + PIECE * n, 8), PIECE)]
        number = 3 * (i - 1) + n
        to = lax.rem(g + i, 4)
        return remote(rows, rows, grp_send.at[number], grp_recv.at[number], d, to)

    def to_peer(array, send, recv, i):
        return remote(
            array.at[0], array.at[i], send.at[i - 1], recv.at[i - 1], d, lax.rem(g + i, 4)
        )

    sends = [message(g, i, n) for n in range(OWN // PIECE) for i in (2, 1, 3)]
    slot_sends = [to_peer(slots, slot_send, slot_recv, i) for i in (2, 1, 3)]
    extra_sends = [to_peer(extra, extra_send, extra_recv, i) for i in (1, 2, 3)]

    def send_parts():
        shared[1] = cond_ref[OWN:SLOTS, :]

        @pl.when(jnp.logical_and(has_above, not_tail))
        def _():
            shared[0] = cond_ref[INNER:OWN, :]
            part_up.start()

        @pl.when(has_below)
        def _():
            part_down.start()

    @pl.when(has_below)
    def _():
        ready_late = prepare_late(faces, pick, back, turn, OWN)
        places, named, face, turn_j, turn_jk, back_jk, slot_row = ready_late

        @pl.when(ahead)
        def _():
            own_coarse()
            slots[0] = slot_row
            pl.semaphore_wait(hello_back, 1)
            for copy in sends:
                copy.start()
            for copy in slot_sends:
                copy.start()

        @pl.when(not_tail)
        def _():
            late_part(ready_late)

        @pl.when(after_ahead)
        def _():
            pl.semaphore_wait(hello, 3)
            pl.semaphore_signal(hello_back, inc=1, device_id=(d - 1, g), device_id_type=MESH)

        @pl.when(ahead)
        def _():
            more = project_late(turn_jk, late_result)
            for v in range(3):
                extra[0, :, v * 128 : (v + 1) * 128] = more[v]
            for copy in extra_sends:
                copy.start()

        late_to_slots(turn_jk, late_result, late_rows)
        add_rows(back_jk, late_rows, cond_ref, INNER, SLOTS)
        send_parts()
        add_rows(back_jk, late_rows, cond_ref, 0, INNER)

    @pl.when(jnp.logical_not(has_below))
    def _():
        send_parts()

    low = project(lambda n: cond_ref[OWN:SLOTS, n * 128 : (n + 1) * 128])
    for v in range(3):
        low_out[:, v * 128 : (v + 1) * 128] = low[v]

    @pl.when(has_below)
    def _():
        @pl.when(jnp.logical_not(after_ahead))
        def _():
            pl.semaphore_wait(hello, 3)

        for copy in low_down:
            copy.start()

    @pl.when(jnp.logical_not(ahead))
    def _():
        own_coarse()
        for copy in sends:
            copy.start()

    @pl.when(has_above)
    def _():
        part_down.wait_recv()
        cond_ref[INNER:OWN, :] = shared[0] + arrived[1]

    @pl.when(has_below)
    def _():
        part_up.wait_recv()
        cond_ref[OWN:SLOTS, :] = shared[1] + arrived[0]

    for copy in sends:
        copy.wait_send()
    for i in range(1, 4):
        for n in range(OWN // PIECE):
            message(lax.rem(g + 4 - i, 4), i, n).wait_recv()

    @pl.when(has_above)
    def _():
        for i in range(4):
            low_down[i].wait_recv()
            owner = lax.rem(g + 4 - i, 4)
            rows = pl.ds(pl.multiple_of(owner * OWN + INNER, 8), 8)
            coarse_ref[rows, :] = coarse_ref[rows, :] - low_in[i]

    @pl.when(ahead)
    def _():
        for copy in slot_sends:
            copy.wait()
        for i in (0, 3, 2, 1):
            if i:
                to_peer(extra, extra_send, extra_recv, i).wait_recv()
            rows = pl.ds(pl.multiple_of(lax.rem(g + 4 - i, 4) * OWN, 8), OWN)
            target = iota((OWN, 128), 0).astype(F32) == slots[i, 0:1, :]
            high, low = split(extra[i])
            more = dot(
                target.astype(F32).astype(BF16)[:, :64], jnp.concatenate([high, low], axis=0)
            )
            coarse_ref[rows, :] = coarse_ref[rows, :] - more
        for copy in extra_sends:
            copy.wait_send()

    @pl.when(has_above)
    def _():
        trace_up.wait_send()
        part_up.wait_send()

    @pl.when(has_below)
    def _():
        part_down.wait_send()
        for copy in low_down:
            copy.wait_send()


def write_out(cond, coarse, cond_out, coarse_out, sem):
    copies = []
    for half in range(2):
        rows = pl.ds(half * 40, 40)
        copies.append(pltpu.make_async_copy(cond.at[rows], cond_out.at[rows], sem.at[half]))
        rows = pl.ds(half * 144, 144)
        copies.append(pltpu.make_async_copy(coarse.at[rows], coarse_out.at[rows], sem.at[2 + half]))
    for copy in copies:
        copy.start()
    for copy in copies:
        copy.wait()


def body(trace, rhs, stiffness, elem_faces, orient, counts):
    n_dom = lax.axis_size("dom")
    matrix = stiffness.reshape(4, 8, 200, 128).transpose(0, 2, 1, 3)
    hbm = pl.BlockSpec(memory_space=pl.ANY)
    vmem = pl.BlockSpec(memory_space=pltpu.VMEM)
    dma = pltpu.SemaphoreType.DMA
    cond, coarse = pl.pallas_call(
        lambda *refs: kernel(n_dom, *refs),
        out_shape=(
            pltpu.VMEM((SLOTS, ROW), F32),
            pltpu.VMEM((4 * OWN, COARSE), F32),
        ),
        in_specs=[hbm] * 5,
        out_specs=(vmem, vmem),
        scratch_shapes=[
            pltpu.VMEM((SLOTS, ROW), F32),
            pltpu.VMEM((8, ROW), F32),
            pltpu.VMEM((OWN, ROW), F32),
            pltpu.VMEM((ELEMS, 200, 128), F32),
            pltpu.VMEM((4, ELEMS), jnp.int32),
            pltpu.VMEM((4, ELEMS), jnp.int32),
            pltpu.VMEM((128, 256), BF16),
            pltpu.VMEM((128, 256), BF16),
            pltpu.VMEM((128, 128), F32),
            pltpu.VMEM((256, ROW), BF16),
            pltpu.VMEM((ELEMS * 160, 128), F32),
            pltpu.VMEM((ELEMS * 40, 128), F32),
            pltpu.VMEM((8 * 40, 128), F32),
            pltpu.VMEM((8 * 40, 128), F32),
            pltpu.VMEM((32, ROW), F32),
            pltpu.VMEM((8, ROW), F32),
            pltpu.VMEM((8, 208, 256), BF16),
            pltpu.VMEM((4, 8, 128), F32),
            pltpu.VMEM((4, 32, COARSE), F32),
            pltpu.VMEM((2, 8, ROW), F32),
            pltpu.VMEM((2, 8, ROW), F32),
            pltpu.VMEM((8, COARSE), F32),
            pltpu.VMEM((4, 8, COARSE), F32),
            dma((4,)),
            dma((ELEMS,)),
            dma((3,)),
            dma((3,)),
            dma((4,)),
            dma((4,)),
            dma((9,)),
            dma((9,)),
            pltpu.SemaphoreType.REGULAR,
            pltpu.SemaphoreType.REGULAR,
            dma((3,)),
            dma((3,)),
            dma((3,)),
            dma((3,)),
        ],
        compiler_params=pltpu.CompilerParams(
            collective_id=0, has_side_effects=True, vmem_limit_bytes=62_488_000
        ),
    )(
        trace[0, 0],
        rhs[0, 0],
        matrix,
        elem_faces[0, 0].T,
        orient[0, 0].T,
    )
    cond, coarse = pl.pallas_call(
        write_out,
        out_shape=(
            jax.ShapeDtypeStruct((SLOTS, ROW), F32),
            jax.ShapeDtypeStruct((4 * OWN, COARSE), F32),
        ),
        in_specs=[vmem] * 2,
        out_specs=(hbm, hbm),
        scratch_shapes=[dma((4,))],
        compiler_params=pltpu.CompilerParams(vmem_limit_bytes=16 * 2**20),
    )(cond, coarse)
    return cond[None, None], coarse[None]


def solution(mesh):
    part = P("dom", "grp", None, None)
    return jax.shard_map(
        body,
        mesh=mesh,
        in_specs=(part, part, part, part, part, P("dom", "grp")),
        out_specs=(part, P("dom", None, None)),
        check_vma=False,
    )
```
